512 devices in a mesh: snd: 64 (over y, z), rcv: 8 (over x, core).
Axes of the slice: x: 4, y: 8, z: 8, core: 2. Of those that a mesh axis runs over, the one named last changes fastest.
Arguments:
- tile_counts: bfloat16 [64, 8, 32, 256, 256], P('snd', 'rcv'), may hold values from 0 to 10, as said below
- tile_sender: int32 [64, 8, 32], P('snd', 'rcv'), may hold values from 0 to 3
- tile_receiver: int32 [64, 8, 32], P('snd', 'rcv'), may hold values from 0 to 31
- tile_action: int32 [64, 8, 32], P('snd', 'rcv'), may hold values from 0 to 255
- tile_fill: int32 [64, 8], P('snd', 'rcv'), may hold values from 1 to 32, as said below
- sender_log_shape: float32 [64, 96, 1024], P('snd', None, 'rcv'), may hold values from -0.5 to 3
- sender_log_rate: float32 [64, 96, 1024], P('snd', None, 'rcv')
- receiver_log_shape: float32 [8, 96, 8192], P('rcv', None, 'snd'), may hold values from -0.5 to 3
- receiver_log_rate: float32 [8, 96, 8192], P('rcv', None, 'snd')
- action_log_shape: float32 [96, 256], replicated, may hold values from -0.5 to 3
- action_log_rate: float32 [96, 256], replicated
Outputs:
- new_sender_log_shape: float32 [64, 96, 1024], P('snd', None, 'rcv')
- new_sender_log_rate: float32 [64, 96, 1024], P('snd', None, 'rcv')
- new_receiver_log_shape: float32 [8, 96, 8192], P('rcv', None, 'snd')
- new_receiver_log_rate: float32 [8, 96, 8192], P('rcv', None, 'snd')
- new_action_log_shape: float32 [96, 256], replicated
- new_action_log_rate: float32 [96, 256], replicated
The draws below stay inside these ranges and needn't reach their ends.
Inputs may be any that keep to these rules, and one draw needn't show every extreme that they name: tile_fill[p, q] is the number of live slots of that device, its first slots; slots beyond it are ignored. In every draw some device has all 32 slots live. `tile_counts`: non-negative weighted counts; many entries are zero.
All inputs are finite; a program needn't handle non-finite values.
Results may differ from the reference program's by a relative error of at most 0.004.
Values may be sent and summed in bfloat16 or wider, within the bound.
A program may use at most 64 MiB of HBM per device.

```python
import math
import jax
import jax.numpy as jnp
import numpy as np
from jax import lax

K = 96
A = 256
BLK = 256
TILE_DEV = 32
SG = 1024
RG = 8192
SB_GRP = 4
RB_GRP = 32
NS = 65536
NR = 65536
N_SND = 64
N_RCV = 8


def ramp_rates(key, lead_size, span_cols, by_lead):
    jitter = jax.random.uniform(key, (lead_size, K, span_cols), jnp.float32, -1.0, 1.0)
    rise_log = math.log(3.0)
    lead_pos = jnp.arange(lead_size, dtype=jnp.float32)[:, None, None]
    col_pos = jnp.arange(span_cols, dtype=jnp.float32)[None, None, :]
    if by_lead:
        position = (lead_pos * span_cols + col_pos) / (lead_size * span_cols)
    else:
        position = col_pos / span_cols + 0.0 * lead_pos
    return jitter - rise_log * position


def draw_sender_log_rate(key, part):
    return math.log(NS) + ramp_rates(jax.random.fold_in(key, 11), N_SND, SG, True)


def draw_receiver_log_rate(key, part):
    return math.log(NR) + ramp_rates(jax.random.fold_in(key, 13), N_RCV, RG, False)


def draw_action_log_rate(key, part):
    jitter = jax.random.uniform(jax.random.fold_in(key, 17), (K, A), jnp.float32, -1.0, 1.0)
    log_base = math.log(64.0 * A) - 0.5 * math.log(float(NS) * float(NR))
    return log_base + jitter


def draw_tile_counts(key, part):
    full_shape = (N_SND, N_RCV, TILE_DEV, BLK, BLK)
    tile_scale = jnp.exp(jax.random.uniform(jax.random.fold_in(key, 21), (N_SND, N_RCV, TILE_DEV, 1, 1), jnp.float32, math.log(0.05), math.log(5.0)))
    uniform_base = jax.random.uniform(jax.random.fold_in(key, 23), full_shape, jnp.float32, 0.0, 2.0)
    values = jnp.maximum(uniform_base - 1.0, 0.0) * 2.0
    return (values * tile_scale).astype(jnp.bfloat16)


def draw_tile_fill(key, part):
    live_counts = jax.random.randint(jax.random.fold_in(key, 31), (N_SND * N_RCV,), 1, TILE_DEV + 1)
    full_slot = jax.random.randint(jax.random.fold_in(key, 37), (), 0, N_SND * N_RCV)
    flat_counts = jnp.where(jnp.arange(N_SND * N_RCV) == full_slot, TILE_DEV, live_counts)
    return flat_counts.reshape(N_SND, N_RCV).astype(jnp.int32)


def touch_ends(values, own_key, low, top_value):
    place = [jax.random.randint(jax.random.fold_in(own_key, axis), (), 0, length) for axis, length in enumerate(values.shape)]
    main_axis = values.shape.index(max(values.shape))
    beside = place[:main_axis] + [(place[main_axis] + 1) % values.shape[main_axis]] + place[main_axis + 1:]
    return values.at[tuple(place)].set(low).at[tuple(beside)].set(top_value)


def block_scale(own_key, extent, cuts, least, high):
    factor_of, own = 1.0, jax.random.fold_in(own_key, 6)
    for dim, blocks in cuts:
        heights = jnp.exp(jax.random.uniform(jax.random.fold_in(own, dim), (blocks,), jnp.float32, least / len(cuts), high / len(cuts)))
        factor_of = factor_of * jnp.repeat(heights, extent[dim] // blocks).reshape([-1 if axis == dim else 1 for axis in range(len(extent))])
    return factor_of


def rank_bounds(count, slope):
    portions = [(1 << 20) // math.isqrt(grade ** slope) + 1 for grade in range(1, count + 1)]
    width = 1 + sum(portions) // (1 << 30)
    return np.cumsum(np.array([max(1, weight // width) for weight in portions]))


def ranked(own_key, extent, count, skew):
    table = rank_bounds(count, skew)
    pick = jax.random.randint(jax.random.fold_in(own_key, 1), extent, 0, int(table[count - 1]))
    rank = jnp.searchsorted(jnp.asarray(table, jnp.int32), pick, side="right")
    return jax.random.permutation(jax.random.fold_in(own_key, 2), count)[rank].astype(jnp.int32)


def setup_inputs(seed: int = 0) -> dict:
    seeds = jax.random.split(jax.random.key(seed), 12)
    return {
        "tile_counts": draw_tile_counts(jax.random.fold_in(seeds[11], 71), 0),
        "tile_sender": touch_ends(jax.random.randint(seeds[1], (N_SND, N_RCV, TILE_DEV), 0, SB_GRP), jax.random.fold_in(seeds[1], 1), 0, SB_GRP - 1).astype(jnp.int32),
        "tile_receiver": touch_ends(ranked(seeds[2], (N_SND, N_RCV, TILE_DEV), RB_GRP, 2), jax.random.fold_in(seeds[2], 3), 0, RB_GRP - 1).astype(jnp.int32),
        "tile_action": touch_ends(ranked(seeds[3], (N_SND, N_RCV, TILE_DEV), A, 2), jax.random.fold_in(seeds[3], 3), 0, A - 1).astype(jnp.int32),
        "tile_fill": draw_tile_fill(jax.random.fold_in(seeds[11], 71), 0),
        "sender_log_shape": jnp.clip(-0.5 + 3.5 * jax.random.uniform(seeds[5], (N_SND, K, SG), jnp.float32) ** block_scale(seeds[5], (N_SND, K, SG), ((0, 64), (2, 8)), -0.2, 0.2), -0.5, 3.0),
        "sender_log_rate": draw_sender_log_rate(jax.random.fold_in(seeds[11], 71), 0),
        "receiver_log_shape": jnp.clip(-0.5 + 3.5 * jax.random.uniform(seeds[7], (N_RCV, K, RG), jnp.float32) ** block_scale(seeds[7], (N_RCV, K, RG), ((0, 8), (2, 64)), -0.2, 0.2), -0.5, 3.0),
        "receiver_log_rate": draw_receiver_log_rate(jax.random.fold_in(seeds[11], 71), 0),
        "action_log_shape": jnp.clip(jax.random.uniform(seeds[9], (K, A), jnp.float32, -0.5, 3.0), -0.5, 3.0),
        "action_log_rate": draw_action_log_rate(jax.random.fold_in(seeds[11], 71), 0),
    }


prior_shape = 0.3
prior_rate = 0.3
step_size = 0.5


def digamma_series(value):
    shift_sum = jnp.zeros_like(value)
    for offset in range(6):
        shift_sum = shift_sum + 1.0 / (value + float(offset))
    moved = value + 6.0
    inverse = 1.0 / moved
    inv_square = inverse * inverse
    series = jnp.log(moved) - 0.5 * inverse - inv_square * (1.0 / 12.0 - inv_square * (1.0 / 120.0 - inv_square / 252.0))
    return series - shift_sum


def geometric(log_shape, log_rate):
    return jnp.exp(digamma_series(jnp.exp(log_shape)) - log_rate)


def refresh(log_value, target):
    return jnp.log((1.0 - step_size) * jnp.exp(log_value) + step_size * target)


def add_columns(running, addend, start_col):
    span_cols = addend.shape[1]
    current = lax.dynamic_slice_in_dim(running, start_col, span_cols, 1)
    return lax.dynamic_update_slice_in_dim(running, current + addend, start_col, 1)


def reference(tile_counts, tile_sender, tile_receiver, tile_action, tile_fill, sender_log_shape, sender_log_rate, receiver_log_shape, receiver_log_rate, action_log_shape, action_log_rate):
    sender_geo = geometric(sender_log_shape, sender_log_rate).astype(jnp.bfloat16)
    receiver_geo = geometric(receiver_log_shape, receiver_log_rate).astype(jnp.bfloat16)
    action_geo = geometric(action_log_shape, action_log_rate)

    def per_device(totals, device_id):
        send_stat, recv_stat, act_stat = totals
        snd_index = device_id // N_RCV
        rcv_index = device_id % N_RCV
        group_send = sender_geo[snd_index]
        group_recv = receiver_geo[rcv_index]
        live_count = tile_fill[snd_index, rcv_index]

        def per_tile(tile_totals, tile_item):
            send_term, recv_term, act_term = tile_totals
            count_tile, send_id, recv_id, act_id, slot_id = tile_item
            live_flag = (slot_id < live_count).astype(jnp.float32)
            send_cols = lax.dynamic_slice_in_dim(group_send, send_id * BLK, BLK, 1)
            recv_cols = lax.dynamic_slice_in_dim(group_recv, recv_id * BLK, BLK, 1)
            act_col = lax.dynamic_slice_in_dim(action_geo, act_id, 1, 1)
            scaled = (send_cols.astype(jnp.float32) * act_col).astype(jnp.bfloat16)
            expected = jnp.dot(scaled.T, recv_cols, preferred_element_type=jnp.float32)
            ratios = (count_tile.astype(jnp.float32) * live_flag / expected).astype(jnp.bfloat16)
            toward_send = jnp.dot(recv_cols, ratios.T, preferred_element_type=jnp.float32)
            toward_recv = jnp.dot(scaled, ratios, preferred_element_type=jnp.float32)
            send_part = scaled.astype(jnp.float32) * toward_send
            recv_part = recv_cols.astype(jnp.float32) * toward_recv
            act_part = jnp.sum(send_part, axis=1, keepdims=True)
            send_term = add_columns(send_term, send_part, send_id * BLK)
            recv_term = add_columns(recv_term, recv_part, recv_id * BLK)
            act_term = add_columns(act_term, act_part, act_id)
            return (send_term, recv_term, act_term), None

        initial = (jnp.zeros((K, SG), jnp.float32), jnp.zeros((K, RG), jnp.float32), jnp.zeros((K, A), jnp.float32))
        items = (tile_counts[snd_index, rcv_index], tile_sender[snd_index, rcv_index], tile_receiver[snd_index, rcv_index], tile_action[snd_index, rcv_index], jnp.arange(TILE_DEV, dtype=jnp.int32))
        (send_term, recv_term, act_term), unused = lax.scan(per_tile, initial, items)
        send_stat = send_stat.at[snd_index].add(send_term)
        recv_stat = recv_stat.at[rcv_index].add(recv_term)
        return (send_stat, recv_stat, act_stat + act_term), None

    start_totals = (jnp.zeros((N_SND, K, SG), jnp.float32), jnp.zeros((N_RCV, K, RG), jnp.float32), jnp.zeros((K, A), jnp.float32))
    (send_stat, recv_stat, act_stat), unused = lax.scan(per_device, start_totals, jnp.arange(N_SND * N_RCV, dtype=jnp.int32))
    sender_total = jnp.sum(jnp.exp(sender_log_shape - sender_log_rate), axis=(0, 2))
    receiver_total = jnp.sum(jnp.exp(receiver_log_shape - receiver_log_rate), axis=(0, 2))
    action_total = jnp.sum(jnp.exp(action_log_shape - action_log_rate), axis=1)
    new_sender_log_shape = refresh(sender_log_shape, prior_shape + send_stat)
    new_sender_log_rate = refresh(sender_log_rate, (prior_rate + receiver_total * action_total)[None, :, None])
    new_receiver_log_shape = refresh(receiver_log_shape, prior_shape + recv_stat)
    new_receiver_log_rate = refresh(receiver_log_rate, (prior_rate + sender_total * action_total)[None, :, None])
    new_action_log_shape = refresh(action_log_shape, prior_shape + act_stat)
    new_action_log_rate = refresh(action_log_rate, (prior_rate + sender_total * receiver_total)[:, None])
    return (new_sender_log_shape, new_sender_log_rate, new_receiver_log_shape, new_receiver_log_rate, new_action_log_shape, new_action_log_rate)
```

```python
import functools

import jax
import jax.numpy as jnp
from jax import lax
from jax.experimental import pallas as pl
from jax.experimental.pallas import tpu as pltpu
from jax.sharding import PartitionSpec as P

prior_shape = 0.3
prior_rate = 0.3
step_size = 0.5
lanes = 128
unroll = 4

MESH = pl.DeviceIdType.MESH
bf16 = jnp.bfloat16
f32 = jnp.float32


def digamma_series(value):
    shift_sum = jnp.zeros_like(value)
    for offset in range(6):
        shift_sum = shift_sum + 1.0 / (value + float(offset))
    moved = value + 6.0
    inverse = 1.0 / moved
    inv_square = inverse * inverse
    series = (
        jnp.log(moved)
        - 0.5 * inverse
        - inv_square * (1.0 / 12.0 - inv_square * (1.0 / 120.0 - inv_square / 252.0))
    )
    return series - shift_sum


def geometric(log_shape, log_rate):
    return jnp.exp(digamma_series(jnp.exp(log_shape)) - log_rate)


def refresh(log_value, target):
    return jnp.log((1.0 - step_size) * jnp.exp(log_value) + step_size * target)


def turned(value):
    rank, cols = value.shape
    padded = jnp.concatenate([value, jnp.zeros((lanes - rank, cols), value.dtype)], axis=0)
    return padded.T


def place(side):
    snd = lax.axis_index("snd")
    return snd // side, lax.rem(snd, side), lax.axis_index("rcv")


def peer_y(y, z, side, offset):
    return {"snd": lax.rem(y + offset + side, side) * side + z}


def peer_z(y, z, side, offset):
    return {"snd": y * side + lax.rem(z + offset + side, side)}


def peer_r(rcv, n_rcv, offset):
    return {"rcv": lax.rem(rcv + offset, n_rcv)}


def greet(side, n_rcv):
    y, z, rcv = place(side)
    barrier = pltpu.get_barrier_semaphore()
    for offset in range(1, side):
        for peer in (peer_y, peer_z):
            pl.semaphore_signal(
                barrier, inc=1, device_id=peer(y, z, side, offset), device_id_type=MESH
            )
    for offset in range(1, n_rcv):
        pl.semaphore_signal(
            barrier, inc=1, device_id=peer_r(rcv, n_rcv, offset), device_id_type=MESH
        )
    return barrier, 2 * (side - 1) + n_rcv - 1


def send(src, dst, send_sem, recv_sem, device):
    copy = pltpu.make_async_remote_copy(
        src_ref=src,
        dst_ref=dst,
        send_sem=send_sem,
        recv_sem=recv_sem,
        device_id=device,
        device_id_type=MESH,
    )
    copy.start()
    return copy


def gather_kernel(
    side,
    n_rcv,
    rs_ref,
    rr_ref,
    ss_ref,
    sr_ref,
    as_ref,
    ar_ref,
    top_ref,
    low_ref,
    sgeo_ref,
    ageo_ref,
    tot_ref,
    near_send,
    near_recv,
    ring_send,
    ring_recv,
    rcv_send,
    rcv_recv,
):
    y, z, rcv = place(side)
    half = side // 2
    barrier, expected = greet(side, n_rcv)
    geo = geometric(rs_ref[0], rr_ref[0]).astype(bf16)
    rows = geo.shape[0] // 2
    top_ref[y, z] = geo[:rows]
    low_ref[z, y] = geo[rows:]
    pl.semaphore_wait(barrier, expected)

    near = []
    for offset in range(1, side):
        for kind in (0, 1):
            ref = (top_ref.at[y, z], low_ref.at[z, y])[kind]
            device = (peer_z, peer_y)[kind](y, z, side, offset)
            near.append(
                send(ref, ref, near_send.at[kind, offset], near_recv.at[kind, offset], device)
            )

    sgeo_ref[rcv] = turned(geometric(ss_ref[0], sr_ref[0])).astype(bf16)
    own = sgeo_ref.at[rcv]
    across = [
        send(own, own, rcv_send.at[o], rcv_recv.at[o], peer_r(rcv, n_rcv, o))
        for o in range(1, n_rcv)
    ]
    send_row = jnp.sum(turned(jnp.exp(ss_ref[0] - sr_ref[0])), axis=0, keepdims=True)
    recv_row = jnp.sum(turned(jnp.exp(rs_ref[0] - rr_ref[0])), axis=0, keepdims=True)
    row_id = lax.broadcasted_iota(jnp.int32, (8, lanes), 0)
    tot_ref[...] = jnp.where(row_id == 0, send_row, jnp.where(row_id == 1, recv_row, 0.0))
    ageo_ref[...] = turned(geometric(as_ref[...], ar_ref[...]))

    for copy in near:
        copy.wait()

    passed = {}
    for step in range(half):
        for piece in (0, 1):
            for kind in (0, 1):
                ref = (top_ref, low_ref)[kind]
                place_id = (y, z)[kind]
                peer = (peer_y, peer_z)[kind]
                for way in (0, 1):
                    if step == half - 1 and piece != way:
                        continue
                    if step > 0:
                        passed[step - 1, piece, kind, way].wait_recv()
                    sign = 1 - 2 * way
                    block = lax.rem(place_id - sign * step + side, side)
                    part = ref.at[block, pl.ds(piece * half, half)]
                    passed[step, piece, kind, way] = send(
                        part,
                        part,
                        ring_send.at[step, piece, kind, way],
                        ring_recv.at[step, piece, kind, way],
                        peer(y, z, side, sign),
                    )
    for (step, piece, kind, way), copy in passed.items():
        forwarded = step < half - 2 or (step == half - 2 and piece == way)
        if not forwarded:
            copy.wait_recv()
        copy.wait_send()
    for copy in across:
        copy.wait()


def tile_kernel(
    side,
    send_id,
    recv_id,
    act_id,
    fill,
    counts_ref,
    top_ref,
    low_ref,
    sgeo_ref,
    ageo_ref,
    top_out,
    low_out,
    send_out,
    act_out,
    counts,
    send_acc,
    recv_acc,
    load_sem,
):
    slots, edge = counts.shape[0], counts.shape[1]
    groups = slots // unroll
    span = edge // lanes
    rows = top_ref.shape[2]

    def load(group):
        part = pl.ds(group * unroll, unroll)
        return pltpu.make_async_copy(
            counts_ref.at[0, 0, part], counts.at[part], load_sem.at[group]
        )

    for group in range(groups):
        load(group).start()
    send_acc[...] = jnp.zeros_like(send_acc)
    act_out[...] = jnp.zeros_like(act_out)

    def clear(block, carry):
        recv_acc[block] = jnp.zeros(recv_acc.shape[1:], f32)
        return carry

    lax.fori_loop(0, recv_acc.shape[0], clear, 0)
    live_count = fill[0]

    def one_tile(slot):
        b, c, a = send_id[slot], recv_id[slot], act_id[slot]
        live = (slot < live_count).astype(f32)
        first = c * span
        y, z = first // side, lax.rem(first, side)
        recv = jnp.concatenate(
            [
                jnp.concatenate([top_ref[y, z + e] for e in range(span)], axis=1),
                jnp.concatenate([low_ref[z + e, y] for e in range(span)], axis=1),
            ],
            axis=0,
        )
        rank = recv.shape[0]
        recv_pad = jnp.concatenate([recv, jnp.zeros((lanes - rank, edge), bf16)], axis=0)
        sender = sgeo_ref[pl.ds(b * span, span)].reshape(edge, lanes)
        scaled = (sender.astype(f32) * ageo_ref[pl.ds(a, 1), :]).astype(bf16)
        expected = jnp.dot(scaled, recv_pad, preferred_element_type=f32)
        ratios = (counts[slot].astype(f32) * live / expected).astype(bf16)
        toward_send = lax.dot_general(
            ratios, recv_pad, (((1,), (1,)), ((), ())), preferred_element_type=f32
        )
        toward_recv = lax.dot_general(
            scaled, ratios, (((0,), (0,)), ((), ())), preferred_element_type=f32
        )
        send_part = scaled.astype(f32) * toward_send
        recv_part = recv.astype(f32) * toward_recv[:rank]
        return b, c, a, send_part, recv_part, jnp.sum(send_part, axis=0, keepdims=True)

    def one_group(group, carry):
        load(group).wait()

        @pl.when(group * unroll < live_count)
        def _():
            done = [one_tile(group * unroll + u) for u in range(unroll)]
            for b, c, a, send_part, recv_part, act_part in done:
                send_acc[pl.ds(b * span, span)] += send_part.reshape(span, lanes, lanes)
                recv_acc[c] += recv_part
                act_out[pl.ds(a, 1), :] += act_part

        return carry

    lax.fori_loop(0, groups, one_group, 0)
    send_out[...] = send_acc[...].astype(bf16)

    def hand_over(block, carry):
        value = recv_acc[block].astype(bf16)
        first = block * span
        y, z = first // side, lax.rem(first, side)
        for e in range(span):
            top_out[y, z + e] = value[:rows, e * lanes : (e + 1) * lanes]
            low_out[z + e, y] = value[rows:, e * lanes : (e + 1) * lanes]
        return carry

    lax.fori_loop(0, recv_acc.shape[0], hand_over, 0)


def reduce_kernel(
    side,
    n_rcv,
    top_ref,
    low_ref,
    send_ref,
    act_ref,
    tot_ref,
    recv_out,
    send_out,
    act_out,
    tot_out,
    ring_src,
    ring_dst,
    near_src,
    near_dst,
    send_dst,
    act_own,
    act_dst,
    sum_src,
    sum_dst,
    ring_send,
    ring_recv,
    near_send,
    near_recv,
    rcv_send,
    rcv_recv,
    sum_send,
    sum_recv,
    back_send,
    back_recv,
):
    y, z, rcv = place(side)
    half = side // 2
    act_rows = act_out.shape[0] // n_rcv
    barrier, expected = greet(side, n_rcv)
    for chunk in range(n_rcv):
        act_own[chunk, :act_rows] = act_ref[pl.ds(chunk * act_rows, act_rows), :]
        act_own[chunk, act_rows:] = tot_ref[...]
    pl.semaphore_wait(barrier, expected)

    refs, where, peers = (top_ref, low_ref), (y, z), (peer_y, peer_z)
    cross = (peer_z, peer_y)
    ring = {}

    def start_ring(step, piece, kind, way, src):
        ring[step, piece, kind, way] = send(
            src,
            ring_dst.at[kind, way, step, piece],
            ring_send.at[step, piece, kind, way],
            ring_recv.at[step, piece, kind, way],
            peers[kind](y, z, side, 1 - 2 * way),
        )

    def block_of(step, kind, way):
        sign = 1 - 2 * way
        return lax.rem(where[kind] + sign * (half - step) + side, side)

    for kind in (0, 1):
        for way in (0, 1):
            for step, piece in ((0, way), (1, 1 - way)):
                part = refs[kind].at[block_of(step, kind, way), pl.ds(piece * half, half)]
                start_ring(step, piece, kind, way, part)

    act_copies, send_copies = [], []
    for o in range(1, n_rcv):
        other = lax.rem(rcv + o, n_rcv)
        act_copies.append(
            send(
                act_own.at[other],
                act_dst.at[rcv],
                rcv_send.at[0, o],
                rcv_recv.at[0, o],
                {"rcv": other},
            )
        )
    for o in range(1, n_rcv):
        other = lax.rem(rcv + o, n_rcv)
        send_copies.append(
            send(
                send_ref.at[other],
                send_dst.at[rcv],
                rcv_send.at[1, o],
                rcv_recv.at[1, o],
                {"rcv": other},
            )
        )
    act_dst[rcv] = act_own[rcv]
    send_dst[rcv] = send_ref[rcv]

    def total_of(ref, count):
        value = ref[0].astype(f32)
        for index in range(1, count):
            value = value + ref[index].astype(f32)
        return value

    def spread(level, value):
        me = where[level]
        sum_src[level] = value
        sum_dst[level, me] = value
        return [
            send(
                sum_src.at[level],
                sum_dst.at[level, me],
                sum_send.at[level, o],
                sum_recv.at[level, o],
                peers[level](y, z, side, o),
            )
            for o in range(1, side)
        ]

    sums = [None, None]
    for step in range(1, half):
        for piece in (0, 1):
            for kind in (0, 1):
                for way in (0, 1):
                    if step == 1 and piece != way:
                        continue
                    ring[step - 1, piece, kind, way].wait_recv()
                    part = refs[kind][block_of(step, kind, way), pl.ds(piece * half, half)]
                    came = ring_dst[kind, way, step - 1, piece]
                    ring_src[kind, way, step - 1, piece] = (
                        part.astype(f32) + came.astype(f32)
                    ).astype(bf16)
                    start_ring(step, piece, kind, way, ring_src.at[kind, way, step - 1, piece])
        if step == 1:
            for copy in act_copies:
                copy.wait()
            sums[0] = spread(0, total_of(act_dst, n_rcv))
        if step == 2:
            for copy in sums[0]:
                copy.wait()
            sums[1] = spread(1, total_of(sum_dst.at[0], side))
    if sums[1] is None:
        for copy in sums[0]:
            copy.wait()
        sums[1] = spread(1, total_of(sum_dst.at[0], side))

    near, held = [], []
    for kind in (0, 1):
        for piece in (0, 1):
            part = refs[kind][where[kind], pl.ds(piece * half, half)].astype(f32)
            for way in (0, 1):
                ring[half - 1, piece, kind, way].wait_recv()
                part = part + ring_dst[kind, way, half - 1, piece].astype(f32)
            near_src[kind, pl.ds(piece * half, half)] = part.astype(bf16)
        mine = where[1 - kind]
        for o in range(1, side):
            other = lax.rem(mine + o, side)
            near.append(
                send(
                    near_src.at[kind, other],
                    near_dst.at[kind, mine],
                    near_send.at[kind, o],
                    near_recv.at[kind, o],
                    cross[kind](y, z, side, o),
                )
            )
        near_dst[kind, mine] = near_src[kind, mine]

    for copy in sums[1]:
        copy.wait()
    full = total_of(sum_dst.at[1], side)
    act_out[pl.ds(rcv * act_rows, act_rows), :] = full[:act_rows]
    tot_out[...] = full[act_rows:]
    own = act_out.at[pl.ds(rcv * act_rows, act_rows), :]
    back = [
        send(own, own, back_send.at[o], back_recv.at[o], peer_r(rcv, n_rcv, o))
        for o in range(1, n_rcv)
    ]
    for copy in send_copies:
        copy.wait()
    send_out[...] = total_of(send_dst, n_rcv)
    for copy in near:
        copy.wait()
    rows = recv_out.shape[0] // 2
    for kind in (0, 1):
        recv_out[kind * rows : (kind + 1) * rows] = total_of(near_dst.at[kind], side)
    for copy in ring.values():
        copy.wait_send()
    for copy in back:
        copy.wait()


def refresh_kernel(
    ss_ref,
    sr_ref,
    rs_ref,
    rr_ref,
    as_ref,
    ar_ref,
    send_ref,
    recv_ref,
    act_ref,
    tot_ref,
    ss_out,
    sr_out,
    rs_out,
    rr_out,
    as_out,
    ar_out,
):
    rank = as_ref.shape[0]
    row = lax.broadcasted_iota(jnp.int32, (rank, lanes), 0)
    col = lax.broadcasted_iota(jnp.int32, (rank, lanes), 1)

    def column(index):
        wide = jnp.broadcast_to(tot_ref[pl.ds(index, 1), :], (rank, lanes))
        return jnp.sum(jnp.where(row == col, wide, 0.0), axis=1, keepdims=True)

    send_total, recv_total = column(0), column(1)
    act_total = jnp.sum(jnp.exp(as_ref[...] - ar_ref[...]), axis=1, keepdims=True)
    ss_out[0] = refresh(ss_ref[0], prior_shape + send_ref[...].T[:rank])
    sr_out[0] = refresh(sr_ref[0], prior_rate + recv_total * act_total)
    rs_out[0] = refresh(rs_ref[0], prior_shape + recv_ref[...])
    rr_out[0] = refresh(rr_ref[0], prior_rate + send_total * act_total)
    as_out[...] = refresh(as_ref[...], prior_shape + act_ref[...].T[:rank])
    ar_out[...] = refresh(ar_ref[...], prior_rate + send_total * recv_total)


def per_device(
    side,
    n_rcv,
    tile_counts,
    tile_sender,
    tile_receiver,
    tile_action,
    tile_fill,
    ss,
    sr,
    rs,
    rr,
    ash,
    art,
):
    rank, actions = ash.shape
    slots, edge = tile_counts.shape[2], tile_counts.shape[3]
    rows, half = rank // 2, side // 2
    vmem = pl.BlockSpec(memory_space=pltpu.VMEM)
    smem = pl.BlockSpec(memory_space=pltpu.SMEM)
    shape = jax.ShapeDtypeStruct
    dma = pltpu.SemaphoreType.DMA

    top, low, sgeo, ageo, tot = pl.pallas_call(
        functools.partial(gather_kernel, side, n_rcv),
        out_shape=(
            shape((side, side, rows, lanes), bf16),
            shape((side, side, rows, lanes), bf16),
            shape((n_rcv, lanes, lanes), bf16),
            shape((actions, lanes), f32),
            shape((8, lanes), f32),
        ),
        in_specs=[vmem] * 6,
        out_specs=(vmem,) * 5,
        scratch_shapes=[
            dma((2, side)),
            dma((2, side)),
            dma((half, 2, 2, 2)),
            dma((half, 2, 2, 2)),
            dma((n_rcv,)),
            dma((n_rcv,)),
        ],
        compiler_params=pltpu.CompilerParams(
            collective_id=0, has_side_effects=True, vmem_limit_bytes=16 << 20
        ),
    )(rs, rr, ss, sr, ash, art)

    blocks = side * side * lanes // edge
    top_part, low_part, send_part, act_part = pl.pallas_call(
        functools.partial(tile_kernel, side),
        out_shape=(
            shape((side, side, rows, lanes), bf16),
            shape((side, side, rows, lanes), bf16),
            shape((n_rcv, lanes, lanes), bf16),
            shape((actions, lanes), f32),
        ),
        in_specs=[smem] * 4 + [pl.BlockSpec(memory_space=pl.ANY)] + [vmem] * 4,
        out_specs=(vmem,) * 4,
        scratch_shapes=[
            pltpu.VMEM((slots, edge, edge), bf16),
            pltpu.VMEM((n_rcv, lanes, lanes), f32),
            pltpu.VMEM((blocks, rank, edge), f32),
            dma((slots // unroll,)),
        ],
        compiler_params=pltpu.CompilerParams(vmem_limit_bytes=32 << 20),
    )(
        tile_sender.reshape(slots),
        tile_receiver.reshape(slots),
        tile_action.reshape(slots),
        tile_fill.reshape(1),
        tile_counts,
        top,
        low,
        sgeo,
        ageo,
    )

    chunk = actions // n_rcv + 8
    recv_stat, send_stat, act_stat, totals = pl.pallas_call(
        functools.partial(reduce_kernel, side, n_rcv),
        out_shape=(
            shape((rank, lanes), f32),
            shape((lanes, lanes), f32),
            shape((actions, lanes), f32),
            shape((8, lanes), f32),
        ),
        in_specs=[vmem] * 5,
        out_specs=(vmem,) * 4,
        scratch_shapes=[
            pltpu.VMEM((2, 2, half - 1, 2, half, rows, lanes), bf16),
            pltpu.VMEM((2, 2, half, 2, half, rows, lanes), bf16),
            pltpu.VMEM((2, side, rows, lanes), bf16),
            pltpu.VMEM((2, side, rows, lanes), bf16),
            pltpu.VMEM((n_rcv, lanes, lanes), bf16),
            pltpu.VMEM((n_rcv, chunk, lanes), f32),
            pltpu.VMEM((n_rcv, chunk, lanes), f32),
            pltpu.VMEM((2, chunk, lanes), f32),
            pltpu.VMEM((2, side, chunk, lanes), f32),
            dma((half, 2, 2, 2)),
            dma((half, 2, 2, 2)),
            dma((2, side)),
            dma((2, side)),
            dma((2, n_rcv)),
            dma((2, n_rcv)),
            dma((2, side)),
            dma((2, side)),
            dma((n_rcv,)),
            dma((n_rcv,)),
        ],
        compiler_params=pltpu.CompilerParams(
            collective_id=1, has_side_effects=True, vmem_limit_bytes=24 << 20
        ),
    )(top_part, low_part, send_part, act_part, tot)

    return pl.pallas_call(
        refresh_kernel,
        out_shape=tuple(shape(x.shape, f32) for x in (ss, sr, rs, rr, ash, art)),
        in_specs=[vmem] * 10,
        out_specs=(vmem,) * 6,
        compiler_params=pltpu.CompilerParams(vmem_limit_bytes=16 << 20),
    )(ss, sr, rs, rr, ash, art, send_stat, recv_stat, act_stat, totals)


def solution(mesh):
    n_snd, n_rcv = mesh.shape["snd"], mesh.shape["rcv"]
    side = round(n_snd**0.5)
    return jax.shard_map(
        functools.partial(per_device, side, n_rcv),
        mesh=mesh,
        in_specs=(
            P("snd", "rcv", None, None, None),
            P("snd", "rcv", None),
            P("snd", "rcv", None),
            P("snd", "rcv", None),
            P("snd", "rcv"),
            P("snd", None, "rcv"),
            P("snd", None, "rcv"),
            P("rcv", None, "snd"),
            P("rcv", None, "snd"),
            P(),
            P(),
        ),
        out_specs=(
            P("snd", None, "rcv"),
            P("snd", None, "rcv"),
            P("rcv", None, "snd"),
            P("rcv", None, "snd"),
            P(),
            P(),
        ),
        check_vma=False,
    )
```

```python
import functools

import jax
import jax.numpy as jnp
from jax import lax
from jax.experimental import pallas as pl
from jax.experimental.pallas import tpu as pltpu
from jax.sharding import PartitionSpec as P

prior_shape = 0.3
prior_rate = 0.3
step_size = 0.5
lanes = 128
unroll = 4
whole_vmem = 60 << 20

MESH = pl.DeviceIdType.MESH
bf16 = jnp.bfloat16
f32 = jnp.float32


def digamma_series(value):
    shift_sum = jnp.zeros_like(value)
    for offset in range(6):
        shift_sum = shift_sum + 1.0 / (value + float(offset))
    moved = value + 6.0
    inverse = 1.0 / moved
    inv_square = inverse * inverse
    series = (
        jnp.log(moved)
        - 0.5 * inverse
        - inv_square * (1.0 / 12.0 - inv_square * (1.0 / 120.0 - inv_square / 252.0))
    )
    return series - shift_sum


def geometric(log_shape, log_rate):
    return jnp.exp(digamma_series(jnp.exp(log_shape)) - log_rate)


def refresh(log_value, target):
    return jnp.log((1.0 - step_size) * jnp.exp(log_value) + step_size * target)


def turned(value):
    rank, cols = value.shape
    padded = jnp.concatenate([value, jnp.zeros((lanes - rank, cols), value.dtype)], axis=0)
    return padded.T


def place(side):
    snd = lax.axis_index("snd")
    return snd // side, lax.rem(snd, side), lax.axis_index("rcv")


def peer_y(y, z, side, offset):
    return {"snd": lax.rem(y + offset + side, side) * side + z}


def peer_z(y, z, side, offset):
    return {"snd": y * side + lax.rem(z + offset + side, side)}


def peer_r(rcv, n_rcv, offset):
    return {"rcv": lax.rem(rcv + offset, n_rcv)}


def greet(side, n_rcv):
    y, z, rcv = place(side)
    barrier = pltpu.get_barrier_semaphore()
    for offset in far_first(side):
        for peer in (peer_y, peer_z):
            pl.semaphore_signal(
                barrier, inc=1, device_id=peer(y, z, side, offset), device_id_type=MESH
            )
    for offset in range(1, n_rcv):
        pl.semaphore_signal(
            barrier, inc=1, device_id=peer_r(rcv, n_rcv, offset), device_id_type=MESH
        )
    return barrier, 2 * (side - 1) + n_rcv - 1


def far_first(side):
    return sorted(range(1, side), key=lambda o: -min(o, side - o))


def slot_of(offset, side):
    return 0 if offset == 0 else (2 * offset - 1 if offset <= side // 2 else 2 * (side - offset))


def slot_at(offset, side):
    offset = lax.rem(offset + side, side)
    near = jnp.maximum(2 * offset - 1, 0)
    return jnp.where(offset <= side // 2, near, 2 * (side - offset))


class Sender:
    def __init__(self, send_sem, recv_sem):
        self.send_sem, self.recv_sem, self.count, self.sent = send_sem, recv_sem, 0, []

    def __call__(self, src, dst, device):
        at = self.count
        self.count += 1
        copy = pltpu.make_async_remote_copy(
            src_ref=src,
            dst_ref=dst,
            send_sem=self.send_sem.at[at // 16, at % 16],
            recv_sem=self.recv_sem.at[at // 16, at % 16],
            device_id=device,
            device_id_type=MESH,
        )
        copy.start()
        self.sent.append(copy)
        return copy


def split3(value):
    high = value.astype(bf16).astype(f32)
    middle = (value - high).astype(bf16).astype(f32)
    return high, middle, value - high - middle


def fused_kernel(
    side,
    n_rcv,
    counts_hbm,
    sid_hbm,
    rid_hbm,
    aid_hbm,
    fill_hbm,
    ss_hbm,
    sr_hbm,
    rs_hbm,
    rr_hbm,
    as_hbm,
    ar_hbm,
    recv_out,
    send_out,
    act_out,
    tot_out,
    ss_ref,
    sr_ref,
    rs_ref,
    rr_ref,
    as_ref,
    ar_ref,
    sid,
    rid,
    aid,
    fill,
    aid_row,
    prev,
    last_recv,
    last_send,
    counts,
    top_ref,
    low_ref,
    sgeo_ref,
    ageo_ref,
    send_slots,
    recv_slots,
    act_rows,
    parts,
    from1,
    from2,
    from3,
    from4,
    joined,
    near_src,
    near_dst,
    send_part,
    send_dst,
    act_own,
    act_dst,
    sum_src,
    sum_dst,
    load_sem,
    count_sem,
    send_sem,
    recv_sem,
):
    y, z, rcv = place(side)
    half = side // 2
    slots, edge = counts.shape[0], counts.shape[1]
    span = edge // lanes
    rank, rows = rs_ref.shape[1], top_ref.shape[2]
    actions = ageo_ref.shape[0]
    blocks, send_blocks = side * side // span, n_rcv // span

    loads = [
        pltpu.make_async_copy(src, dst, load_sem.at[index])
        for index, (src, dst) in enumerate(
            (
                (rs_hbm, rs_ref),
                (rr_hbm, rr_ref),
                (ss_hbm, ss_ref),
                (sr_hbm, sr_ref),
                (as_hbm, as_ref),
                (ar_hbm, ar_ref),
                (sid_hbm, sid),
                (rid_hbm, rid),
                (aid_hbm, aid),
                (fill_hbm, fill),
                (aid_hbm, aid_row),
            )
        )
    ]
    for copy in loads:
        copy.start()
    barrier, greeted = greet(side, n_rcv)
    count_loads = [
        pltpu.make_async_copy(
            counts_hbm.at[0, 0, pl.ds(group * unroll, unroll)],
            counts.at[pl.ds(group * unroll, unroll)],
            count_sem.at[group],
        )
        for group in range(slots // unroll)
    ]
    for copy in count_loads:
        copy.start()
    for copy in loads[:4]:
        copy.wait()
    geo = geometric(rs_ref[0], rr_ref[0]).astype(bf16)
    top_ref[y, 0] = geo[:rows]
    low_ref[z, 0] = geo[rows:]
    sgeo_ref[rcv] = turned(geometric(ss_ref[0], sr_ref[0])).astype(bf16)
    go = Sender(send_sem, recv_sem)
    pl.semaphore_wait(barrier, greeted)

    refs, where = (top_ref, low_ref), (y, z)
    ring_peer, near_peer = (peer_y, peer_z), (peer_z, peer_y)
    pieces = [(at, side // 4) for at in range(0, side, side // 4)]
    near, first, second = {}, {}, []

    def to_ring(kind, distance):
        return ring_peer[kind](y, z, side, distance)

    def step_one(start, size):
        for kind in (0, 1):
            for slot in range(max(start, 1), start + size):
                near[kind, slot].wait_recv()
            part = refs[kind].at[where[kind], pl.ds(start, size)]
            for distance in (2, -2, 1, -1):
                first[kind, start, distance] = go(part, part, to_ring(kind, distance))

    def step_two(start, size):
        for kind in (0, 1):
            for way in (1, -1):
                first[kind, start, 2 * way].wait_recv()
                block = lax.rem(where[kind] - 2 * way + side, side)
                part = refs[kind].at[block, pl.ds(start, size)]
                if (start < half) == (way == 1):
                    second.append(go(part, part, to_ring(kind, 2 * way)))
                second.append(go(part, part, to_ring(kind, way)))

    for offset in far_first(side):
        for kind in (0, 1):
            slot = slot_of(side - offset, side)
            near[kind, slot] = go(
                refs[kind].at[where[kind], 0],
                refs[kind].at[where[kind], slot],
                near_peer[kind](y, z, side, offset),
            )
    own = sgeo_ref.at[rcv]
    across = [go(own, own, peer_r(rcv, n_rcv, o)) for o in range(1, n_rcv)]
    step_one(*pieces[0])
    for index in range(1, len(pieces)):
        step_one(*pieces[index])
        step_two(*pieces[index - 1])
    step_two(*pieces[-1])

    for copy in loads[4:]:
        copy.wait()
    ageo_ref[...] = turned(geometric(as_ref[...], ar_ref[...]))
    send_row = jnp.sum(turned(jnp.exp(ss_ref[0] - sr_ref[0])), axis=0, keepdims=True)
    recv_row = jnp.sum(turned(jnp.exp(rs_ref[0] - rr_ref[0])), axis=0, keepdims=True)
    row_id = lax.broadcasted_iota(jnp.int32, (16, lanes), 0)
    totals = jnp.zeros((16, lanes), f32)
    for index, row in enumerate(split3(send_row) + split3(recv_row)):
        totals = jnp.where(row_id == index, row, totals)
    act_chunk = actions // n_rcv
    for chunk in range(n_rcv):
        act_own[chunk, act_chunk:] = totals
    send_slots[slots] = jnp.zeros(send_slots.shape[1:], f32)
    recv_slots[slots] = jnp.zeros(recv_slots.shape[1:], f32)

    def link(slot, carry):
        b, c = sid[0, 0, slot], rid[0, 0, slot]
        before_b, before_c = jnp.int32(slots), jnp.int32(slots)
        for other in range(slots):
            earlier = other < slot
            before_b = jnp.where((sid[0, 0, other] == b) & earlier, other, before_b)
            before_c = jnp.where((rid[0, 0, other] == c) & earlier, other, before_c)
        prev[0, slot] = before_b
        prev[1, slot] = before_c
        return carry

    def final(ids, table):
        def body(block, carry):
            found = jnp.int32(slots)
            for other in range(slots):
                found = jnp.where(ids[0, 0, other] == block, other, found)
            table[block] = found
            return carry

        return body

    lax.fori_loop(0, slots, link, 0)
    lax.fori_loop(0, blocks, final(rid, last_recv), 0)
    lax.fori_loop(0, send_blocks, final(sid, last_send), 0)

    for (kind, start, distance), copy in first.items():
        if abs(distance) == 1:
            copy.wait_recv()
    for copy in second:
        copy.wait_recv()
    for copy in across:
        copy.wait_recv()
    for copy in count_loads:
        copy.wait()

    live_count = fill[0, 0]

    def one_tile(slot):
        b, c, a = sid[0, 0, slot], rid[0, 0, slot], aid[0, 0, slot]
        live = jnp.where(slot < live_count, 1.0, 0.0).astype(f32)
        begin = c * span
        ty, tz = begin // side, lax.rem(begin, side)
        down = slot_at(ty - y, side)
        recv = jnp.concatenate(
            [
                jnp.concatenate(
                    [top_ref[ty, slot_at(tz + e - z, side)] for e in range(span)], axis=1
                ),
                jnp.concatenate([low_ref[tz + e, down] for e in range(span)], axis=1),
            ],
            axis=0,
        )
        recv_pad = jnp.concatenate([recv, jnp.zeros((lanes - rank, edge), bf16)], axis=0)
        sender = sgeo_ref[pl.ds(b * span, span)].reshape(edge, lanes)
        scaled = (sender.astype(f32) * ageo_ref[pl.ds(a, 1), :]).astype(bf16)
        expected = jnp.dot(scaled, recv_pad, preferred_element_type=f32)
        ratios = (counts[slot].astype(f32) * live / expected).astype(bf16)
        toward_send = lax.dot_general(
            ratios, recv_pad, (((1,), (1,)), ((), ())), preferred_element_type=f32
        )
        toward_recv = lax.dot_general(
            scaled, ratios, (((0,), (0,)), ((), ())), preferred_element_type=f32
        )
        send_term = scaled.astype(f32) * toward_send
        recv_term = recv.astype(f32) * toward_recv[:rank]
        return send_term, recv_term, jnp.sum(send_term, axis=0, keepdims=True)

    def one_group(group, carry):
        done = [one_tile(group * unroll + u) for u in range(unroll)]
        for u, (send_term, recv_term, act_term) in enumerate(done):
            slot = group * unroll + u
            send_slots[slot] = send_term + send_slots[prev[0, slot]]
            recv_slots[slot] = recv_term + recv_slots[prev[1, slot]]
            act_rows[pl.ds(slot, 1), :] = act_term
        return carry

    lax.fori_loop(0, slots // unroll, one_group, 0)

    action_id = lax.broadcasted_iota(jnp.int32, (actions, slots), 0)
    onehot = jnp.where(action_id == aid_row[0], 1.0, 0.0).astype(f32)
    act_sum = jnp.dot(
        onehot, act_rows[...], preferred_element_type=f32, precision=lax.Precision.HIGHEST
    )
    for chunk in range(n_rcv):
        act_own[chunk, :act_chunk] = act_sum[chunk * act_chunk : (chunk + 1) * act_chunk]
    act_copies = []
    for o in range(1, n_rcv):
        other = lax.rem(rcv + o, n_rcv)
        act_copies.append(go(act_own.at[other], act_dst.at[rcv], {"rcv": other}))
    act_dst[rcv] = act_own[rcv]

    def hand_over(block, carry):
        value = recv_slots[last_recv[block]].astype(bf16)
        begin = block * span
        ty, tz = begin // side, lax.rem(begin, side)
        for e in range(span):
            columns = value[:, e * lanes : (e + 1) * lanes]
            parts[0, ty, slot_at(tz + e - z, side)] = columns[:rows]
            parts[1, tz + e, slot_at(ty - y, side)] = columns[rows:]
        return carry

    lax.fori_loop(0, blocks, hand_over, 0)

    came1, came2, came3, came4 = {}, {}, {}, {}

    def block_at(kind, distance):
        return lax.rem(where[kind] + distance + side, side)

    def piece_of(kind, distance, start, size):
        return parts.at[kind, block_at(kind, distance), pl.ds(start, size)]

    backwards = pieces[::-1]
    for start, size in backwards:
        for kind in (0, 1):
            for way in (1, -1):
                at = (kind, (1 - way) // 2, pl.ds(start, size))
                if (start < half) == (way == 1):
                    came4[kind, start, way] = go(
                        piece_of(kind, 4 * way, start, size), from4.at[at], to_ring(kind, 2 * way)
                    )
                came3[kind, start, way] = go(
                    piece_of(kind, 3 * way, start, size), from3.at[at], to_ring(kind, way)
                )
    for start, size in backwards:
        for kind in (0, 1):
            for way in (1, -1):
                at = (kind, (1 - way) // 2, pl.ds(start, size))
                came1[kind, start, way] = go(
                    piece_of(kind, way, start, size), from1.at[at], to_ring(kind, way)
                )

    def give(block, carry):
        value = send_slots[last_send[block]].astype(bf16)
        for e in range(span):
            send_part[block * span + e] = value[e * lanes : (e + 1) * lanes]
        return carry

    lax.fori_loop(0, send_blocks, give, 0)
    send_copies = []
    for o in range(1, n_rcv):
        other = lax.rem(rcv + o, n_rcv)
        send_copies.append(go(send_part.at[other], send_dst.at[rcv], {"rcv": other}))
    send_dst[rcv] = send_part[rcv]

    def join(start, size):
        for kind in (0, 1):
            for way in (1, -1):
                at = (kind, (1 - way) // 2, pl.ds(start, size))
                total = parts[kind, block_at(kind, 2 * way), pl.ds(start, size)].astype(f32)
                came3[kind, start, way].wait_recv()
                total = total + from3[at].astype(f32)
                if (start < half) == (way == 1):
                    came4[kind, start, way].wait_recv()
                    total = total + from4[at].astype(f32)
                joined[at] = total.astype(bf16)
                came2[kind, start, way] = go(joined.at[at], from2.at[at], to_ring(kind, 2 * way))

    def total_of(ref, count):
        value = ref[0].astype(f32)
        for index in range(1, count):
            value = value + ref[index].astype(f32)
        return value

    def spread(level, value):
        me = where[level]
        sum_src[level] = value.astype(bf16)
        sum_dst[level, me] = value.astype(bf16)
        return [
            go(sum_src.at[level], sum_dst.at[level, me], to_ring(level, o))
            for o in far_first(side)
        ]

    def split_totals(value):
        tail = value[act_chunk:]
        result = jnp.zeros_like(tail)
        for base in (0, 3):
            row = tail[base : base + 1] + (tail[base + 1 : base + 2] + tail[base + 2 : base + 3])
            for index, part in enumerate(split3(row)):
                result = jnp.where(row_id == base + index, part, result)
        return jnp.concatenate([value[:act_chunk], result], axis=0)

    near_copies = []

    def finish(start, size):
        for kind in (0, 1):
            total = parts[kind, where[kind], pl.ds(start, size)].astype(f32)
            for way in (1, -1):
                at = (kind, (1 - way) // 2, pl.ds(start, size))
                came1[kind, start, way].wait_recv()
                total = total + from1[at].astype(f32)
                came2[kind, start, way].wait_recv()
                total = total + from2[at].astype(f32)
            near_src[kind, pl.ds(start, size)] = total.astype(bf16)
            for offset in far_first(side):
                slot = slot_of(offset, side)
                if start <= slot < start + size:
                    near_copies.append(
                        go(
                            near_src.at[kind, slot],
                            near_dst.at[kind, slot_of(side - offset, side)],
                            near_peer[kind](y, z, side, offset),
                        )
                    )

    join(*backwards[0])
    join(*backwards[1])
    for copy in act_copies:
        copy.wait_recv()
    sums = spread(0, split_totals(total_of(act_dst, n_rcv)))
    join(*backwards[2])
    join(*backwards[3])
    finish(*backwards[0])
    finish(*backwards[1])
    for copy in sums:
        copy.wait_recv()
    sums = spread(1, split_totals(total_of(sum_dst.at[0], side)))
    finish(*backwards[2])
    finish(*backwards[3])
    for kind in (0, 1):
        near_dst[kind, 0] = near_src[kind, 0]
    for copy in send_copies:
        copy.wait_recv()
    send_out[...] = total_of(send_dst, n_rcv)
    for copy in sums:
        copy.wait_recv()
    full = total_of(sum_dst.at[1], side)
    act_out[pl.ds(rcv * act_chunk, act_chunk), :] = full[:act_chunk]
    own = act_out.at[pl.ds(rcv * act_chunk, act_chunk), :]
    back = [go(own, own, peer_r(rcv, n_rcv, o)) for o in range(1, n_rcv)]
    tot_out[...] = full[act_chunk:]
    for copy in near_copies:
        copy.wait_recv()
    for kind in (0, 1):
        recv_out[kind * rows : (kind + 1) * rows] = total_of(near_dst.at[kind], side)
    for copy in back:
        copy.wait_recv()
    for copy in go.sent:
        copy.wait_send()


def refresh_kernel(*refs):
    sources, outs, refs = refs[:10], refs[10:16], refs[16:]
    held, load_sem = refs[:10], refs[10]
    for index in range(10):
        pltpu.make_async_copy(sources[index], held[index], load_sem.at[index]).start()
    for index in range(10):
        pltpu.make_async_copy(sources[index], held[index], load_sem.at[index]).wait()
    ss_ref, sr_ref, rs_ref, rr_ref, as_ref, ar_ref, send_ref, recv_ref, act_ref, tot_ref = held
    ss_out, sr_out, rs_out, rr_out, as_out, ar_out = outs
    rank = as_ref.shape[0]
    row = lax.broadcasted_iota(jnp.int32, (rank, lanes), 0)
    col = lax.broadcasted_iota(jnp.int32, (rank, lanes), 1)

    def column(index):
        parts = [tot_ref[pl.ds(index + part, 1), :] for part in range(3)]
        wide = jnp.broadcast_to(parts[0] + (parts[1] + parts[2]), (rank, lanes))
        return jnp.sum(jnp.where(row == col, wide, 0.0), axis=1, keepdims=True)

    send_total, recv_total = column(0), column(3)
    act_total = jnp.sum(jnp.exp(as_ref[...] - ar_ref[...]), axis=1, keepdims=True)
    ss_out[0] = refresh(ss_ref[0], prior_shape + send_ref[...].T[:rank])
    sr_out[0] = refresh(sr_ref[0], prior_rate + recv_total * act_total)
    rs_out[0] = refresh(rs_ref[0], prior_shape + recv_ref[...])
    rr_out[0] = refresh(rr_ref[0], prior_rate + send_total * act_total)
    as_out[...] = refresh(as_ref[...], prior_shape + act_ref[...].T[:rank])
    ar_out[...] = refresh(ar_ref[...], prior_rate + send_total * recv_total)


def per_device(
    side,
    n_rcv,
    tile_counts,
    tile_sender,
    tile_receiver,
    tile_action,
    tile_fill,
    ss,
    sr,
    rs,
    rr,
    ash,
    art,
):
    rank, actions = ash.shape
    slots, edge = tile_counts.shape[2], tile_counts.shape[3]
    rows, span = rank // 2, edge // lanes
    blocks, send_blocks = side * side // span, n_rcv // span
    vmem = pl.BlockSpec(memory_space=pltpu.VMEM)
    hbm = pl.BlockSpec(memory_space=pltpu.HBM)
    shape = jax.ShapeDtypeStruct
    dma = pltpu.SemaphoreType.DMA
    own, act = pltpu.VMEM(ss.shape, f32), pltpu.VMEM(ash.shape, f32)
    ids = pltpu.SMEM(tile_sender.shape, jnp.int32)
    geo = pltpu.VMEM((side, side, rows, lanes), bf16)
    landing = pltpu.VMEM((2, 2, side, rows, lanes), bf16)
    near = pltpu.VMEM((2, side, rows, lanes), bf16)
    sender = pltpu.VMEM((n_rcv, lanes, lanes), bf16)
    chunk = actions // n_rcv + 16

    recv_stat, send_stat, act_stat, totals = pl.pallas_call(
        functools.partial(fused_kernel, side, n_rcv),
        out_shape=(
            shape((rank, lanes), f32),
            shape((lanes, lanes), f32),
            shape((actions, lanes), f32),
            shape((16, lanes), f32),
        ),
        in_specs=[hbm] * 11,
        out_specs=(vmem,) * 4,
        scratch_shapes=[
            own,
            own,
            own,
            own,
            act,
            act,
            ids,
            ids,
            ids,
            pltpu.SMEM(tile_fill.shape, jnp.int32),
            pltpu.VMEM(tile_action.shape, jnp.int32),
            pltpu.SMEM((2, slots), jnp.int32),
            pltpu.SMEM((blocks,), jnp.int32),
            pltpu.SMEM((send_blocks,), jnp.int32),
            pltpu.VMEM((slots, edge, edge), bf16),
            geo,
            geo,
            sender,
            pltpu.VMEM((actions, lanes), f32),
            pltpu.VMEM((slots + 1, edge, lanes), f32),
            pltpu.VMEM((slots + 1, rank, edge), f32),
            pltpu.VMEM((slots, lanes), f32),
            pltpu.VMEM((2, side, side, rows, lanes), bf16),
            landing,
            landing,
            landing,
            landing,
            landing,
            near,
            near,
            sender,
            sender,
            pltpu.VMEM((n_rcv, chunk, lanes), f32),
            pltpu.VMEM((n_rcv, chunk, lanes), f32),
            pltpu.VMEM((2, chunk, lanes), bf16),
            pltpu.VMEM((2, side, chunk, lanes), bf16),
            dma((11,)),
            dma((slots // unroll,)),
            dma((16, 16)),
            dma((16, 16)),
        ],
        compiler_params=pltpu.CompilerParams(
            collective_id=0, has_side_effects=True, vmem_limit_bytes=whole_vmem
        ),
    )(
        tile_counts,
        tile_sender,
        tile_receiver,
        tile_action,
        tile_fill,
        ss,
        sr,
        rs,
        rr,
        ash,
        art,
    )

    sources = (ss, sr, rs, rr, ash, art, send_stat, recv_stat, act_stat, totals)
    return pl.pallas_call(
        refresh_kernel,
        out_shape=tuple(shape(x.shape, f32) for x in (ss, sr, rs, rr, ash, art)),
        in_specs=[hbm] * len(sources),
        out_specs=(vmem,) * 6,
        scratch_shapes=[pltpu.VMEM(x.shape, f32) for x in sources] + [dma((len(sources),))],
        compiler_params=pltpu.CompilerParams(vmem_limit_bytes=whole_vmem),
    )(*sources)


def solution(mesh):
    n_snd, n_rcv = mesh.shape["snd"], mesh.shape["rcv"]
    side = round(n_snd**0.5)
    return jax.shard_map(
        functools.partial(per_device, side, n_rcv),
        mesh=mesh,
        in_specs=(
            P("snd", "rcv", None, None, None),
            P("snd", "rcv", None),
            P("snd", "rcv", None),
            P("snd", "rcv", None),
            P("snd", "rcv"),
            P("snd", None, "rcv"),
            P("snd", None, "rcv"),
            P("rcv", None, "snd"),
            P("rcv", None, "snd"),
            P(),
            P(),
        ),
        out_specs=(
            P("snd", None, "rcv"),
            P("snd", None, "rcv"),
            P("rcv", None, "snd"),
            P("rcv", None, "snd"),
            P(),
            P(),
        ),
        check_vma=False,
    )
```

```python
import functools

import jax
import jax.numpy as jnp
from jax import lax
from jax.experimental import pallas as pl
from jax.experimental.pallas import tpu as pltpu
from jax.sharding import PartitionSpec as P

prior_shape = 0.3
prior_rate = 0.3
step_size = 0.5
lanes = 128
unroll = 8
whole_vmem = 60 << 20

MESH = pl.DeviceIdType.MESH
bf16 = jnp.bfloat16
f32 = jnp.float32


def digamma_series(value):
    shift_sum = jnp.zeros_like(value)
    for offset in range(6):
        shift_sum = shift_sum + 1.0 / (value + float(offset))
    moved = value + 6.0
    inverse = 1.0 / moved
    inv_square = inverse * inverse
    series = (
        jnp.log(moved)
        - 0.5 * inverse
        - inv_square * (1.0 / 12.0 - inv_square * (1.0 / 120.0 - inv_square / 252.0))
    )
    return series - shift_sum


def geometric(log_shape, log_rate):
    return jnp.exp(digamma_series(jnp.exp(log_shape)) - log_rate)


def refresh(log_value, target):
    return jnp.log((1.0 - step_size) * jnp.exp(log_value) + step_size * target)


def turned(value):
    rank, cols = value.shape
    padded = jnp.concatenate([value, jnp.zeros((lanes - rank, cols), value.dtype)], axis=0)
    return padded.T


def place(side):
    snd = lax.axis_index("snd")
    return snd // side, lax.rem(snd, side), lax.axis_index("rcv")


def peer_y(y, z, side, offset):
    return {"snd": lax.rem(y + offset + side, side) * side + z}


def peer_z(y, z, side, offset):
    return {"snd": y * side + lax.rem(z + offset + side, side)}


def peer_r(rcv, n_rcv, offset):
    return {"rcv": lax.rem(rcv + offset, n_rcv)}


def greet(side, n_rcv):
    y, z, rcv = place(side)
    barrier = pltpu.get_barrier_semaphore()
    for offset in far_first(side):
        for peer in (peer_y, peer_z):
            pl.semaphore_signal(
                barrier, inc=1, device_id=peer(y, z, side, offset), device_id_type=MESH
            )
    for offset in range(1, n_rcv):
        pl.semaphore_signal(
            barrier, inc=1, device_id=peer_r(rcv, n_rcv, offset), device_id_type=MESH
        )
    return barrier, 2 * (side - 1) + n_rcv - 1


def far_first(side):
    return sorted(range(1, side), key=lambda o: -min(o, side - o))


def slot_of(offset, side):
    return 0 if offset == 0 else (2 * offset - 1 if offset <= side // 2 else 2 * (side - offset))


def slot_at(offset, side):
    offset = lax.rem(offset + side, side)
    near = jnp.maximum(2 * offset - 1, 0)
    return jnp.where(offset <= side // 2, near, 2 * (side - offset))


class Group:
    def __init__(self, sems):
        self.sems = sems

    def start(self, src, dst, device, arrive=None):
        pltpu.make_async_remote_copy(
            src_ref=src,
            dst_ref=dst,
            send_sem=self.sems[0],
            recv_sem=arrive if arrive is not None else self.sems[1],
            device_id=device,
            device_id_type=MESH,
        ).start()


def settle(sem, like):
    pltpu.make_async_copy(like, like, sem).wait()


def split3(value):
    high = value.astype(bf16).astype(f32)
    middle = (value - high).astype(bf16).astype(f32)
    return high, middle, value - high - middle


def fused_kernel(
    side,
    n_rcv,
    counts_hbm,
    sid_hbm,
    rid_hbm,
    aid_hbm,
    fill_hbm,
    ss_hbm,
    sr_hbm,
    rs_hbm,
    rr_hbm,
    as_hbm,
    ar_hbm,
    recv_out,
    send_out,
    act_out,
    tot_out,
    own_ref,
    act_ref,
    ids,
    fill,
    aid_row,
    prev,
    last_recv,
    last_send,
    counts,
    top_ref,
    low_ref,
    sgeo_ref,
    ageo_ref,
    scaled_ref,
    turned_ref,
    send_slots,
    recv_slots,
    act_rows,
    parts,
    from1,
    from2,
    from3,
    from4,
    joined,
    near_src,
    near_dst,
    send_part,
    send_dst,
    act_own,
    act_dst,
    sum_src,
    sum_dst,
    load_sem,
    near_sems,
    ring_send,
    ring_recv,
    rest_recv,
    done_recv,
    last_sems,
    pair_sems,
):
    y, z, rcv = place(side)
    half = side // 2
    slots, edge = counts.shape[0], counts.shape[1]
    span = edge // lanes
    rank, rows = own_ref.shape[1], top_ref.shape[2]
    actions = ageo_ref.shape[0]
    blocks, send_blocks = side * side // span, n_rcv // span

    loads = [
        pltpu.make_async_copy(src, dst, load_sem.at[index])
        for index, src, dst in (
            (0, rs_hbm.at[0], own_ref.at[0]),
            (0, rr_hbm.at[0], own_ref.at[1]),
            (0, ss_hbm.at[0], own_ref.at[2]),
            (0, sr_hbm.at[0], own_ref.at[3]),
            (1, as_hbm, act_ref.at[0]),
            (1, ar_hbm, act_ref.at[1]),
            (2, sid_hbm.at[0], ids.at[0]),
            (2, rid_hbm.at[0], ids.at[1]),
            (2, aid_hbm.at[0], ids.at[2]),
            (3, fill_hbm, fill),
            (4, aid_hbm.at[0], aid_row),
            (5, counts_hbm.at[0, 0], counts),
        )
    ]
    for copy in loads:
        copy.start()
    barrier, greeted = greet(side, n_rcv)
    settle(load_sem.at[0], own_ref)
    geo = geometric(own_ref[0], own_ref[1]).astype(bf16)
    top_ref[y, 0] = geo[:rows]
    low_ref[z, 0] = geo[rows:]
    sgeo_ref[rcv] = turned(geometric(own_ref[2], own_ref[3])).astype(bf16)
    pl.semaphore_wait(barrier, greeted)

    refs, where = (top_ref, low_ref), (y, z)
    ring_peer, near_peer = (peer_y, peer_z), (peer_z, peer_y)
    pieces = ((0, 1), (1, half - 1), (half, side - half))

    def to_ring(kind, distance):
        return ring_peer[kind](y, z, side, distance)

    def block_at(kind, distance):
        return lax.rem(where[kind] + distance + side, side)

    near = [Group((near_sems.at[kind, 0], None)) for kind in (0, 1)]
    ring = [Group((ring_send.at[0, kind], rest_recv.at[kind])) for kind in (0, 1)]

    def forward(index):
        start, size = pieces[index]
        for kind in (0, 1):
            part = refs[kind].at[where[kind], pl.ds(start, size)]
            if start:
                settle(near_sems.at[kind, index], part)
            for way in (0, 1):
                ring[kind].start(
                    part, part, to_ring(kind, 2 - 4 * way), ring_recv.at[0, kind, way, index]
                )

    def onward(index):
        start, size = pieces[index]
        for kind in (0, 1):
            for way in (0, 1):
                sign = 1 - 2 * way
                part = refs[kind].at[block_at(kind, -2 * sign), pl.ds(start, size)]
                settle(ring_recv.at[0, kind, way, index], part)
                if (start < half) == (way == 0):
                    ring[kind].start(part, part, to_ring(kind, 2 * sign))
                ring[kind].start(part, part, to_ring(kind, sign))

    for offset in far_first(side):
        for kind in (0, 1):
            slot = slot_of(side - offset, side)
            near[kind].start(
                refs[kind].at[where[kind], 0],
                refs[kind].at[where[kind], slot],
                near_peer[kind](y, z, side, offset),
                near_sems.at[kind, 1 if slot < half else 2],
            )
    forward(0)
    across = Group((pair_sems.at[0, 0], pair_sems.at[0, 1]))
    for o in range(1, n_rcv):
        across.start(sgeo_ref.at[rcv], sgeo_ref.at[rcv], peer_r(rcv, n_rcv, o))

    settle(load_sem.at[1], act_ref)
    settle(load_sem.at[2], ids)
    ageo_ref[...] = turned(geometric(act_ref[0], act_ref[1]))

    def link(slot, carry):
        b, c = ids[0, 0, slot], ids[1, 0, slot]
        before_b, before_c = jnp.int32(slots), jnp.int32(slots)
        for other in range(slots):
            earlier = other < slot
            before_b = jnp.where((ids[0, 0, other] == b) & earlier, other, before_b)
            before_c = jnp.where((ids[1, 0, other] == c) & earlier, other, before_c)
        prev[0, slot] = before_b
        prev[1, slot] = before_c
        return carry

    def final(row, table):
        def body(block, carry):
            found = jnp.int32(slots)
            for other in range(slots):
                found = jnp.where(ids[row, 0, other] == block, other, found)
            table[block] = found
            return carry

        return body

    lax.fori_loop(0, slots, link, 0)
    for index in range(1, len(pieces)):
        forward(index)
    for index in range(len(pieces)):
        onward(index)
    for kind in (0, 1):
        part = refs[kind].at[where[kind]]
        for sign in (1, -1):
            ring[kind].start(part, part, to_ring(kind, sign))

    settle(pair_sems.at[0, 1], sgeo_ref.at[pl.ds(0, n_rcv - 1)])

    def scale(slot, carry):
        b, a = ids[0, 0, slot], ids[2, 0, slot]
        sender = sgeo_ref[pl.ds(b * span, span)].reshape(edge, lanes)
        scaled = (sender.astype(f32) * ageo_ref[pl.ds(a, 1), :]).astype(bf16)
        scaled_ref[slot] = scaled
        turned_ref[slot] = scaled.T[:rank]
        return carry

    lax.fori_loop(0, slots, scale, 0, unroll=4)
    lax.fori_loop(0, blocks, final(1, last_recv), 0)
    lax.fori_loop(0, send_blocks, final(0, last_send), 0)
    send_row = jnp.sum(turned(jnp.exp(own_ref[2] - own_ref[3])), axis=0, keepdims=True)
    recv_row = jnp.sum(turned(jnp.exp(own_ref[0] - own_ref[1])), axis=0, keepdims=True)
    row_id = lax.broadcasted_iota(jnp.int32, (16, lanes), 0)
    totals = jnp.zeros((16, lanes), f32)
    for index, row in enumerate(split3(send_row) + split3(recv_row)):
        totals = jnp.where(row_id == index, row, totals)
    act_chunk = actions // n_rcv
    for chunk in range(n_rcv):
        act_own[chunk, act_chunk:] = totals.astype(bf16)
    send_slots[slots] = jnp.zeros(send_slots.shape[1:], f32)
    recv_slots[slots] = jnp.zeros(recv_slots.shape[1:], f32)
    settle(load_sem.at[3], fill)
    settle(load_sem.at[4], aid_row)
    settle(load_sem.at[5], counts)
    for kind in (0, 1):
        settle(rest_recv.at[kind], refs[kind].at[pl.ds(0, 5)])

    live_count = fill[0, 0]

    def one_tile(slot):
        c = ids[1, 0, slot]
        live = jnp.where(slot < live_count, 1.0, 0.0).astype(f32)
        begin = c * span
        ty, tz = begin // side, lax.rem(begin, side)
        down = slot_at(ty - y, side)
        recv = jnp.concatenate(
            [
                jnp.concatenate(
                    [top_ref[ty, slot_at(tz + e - z, side)] for e in range(span)], axis=1
                ),
                jnp.concatenate([low_ref[tz + e, down] for e in range(span)], axis=1),
            ],
            axis=0,
        )
        recv_pad = jnp.concatenate([recv, jnp.zeros((lanes - rank, edge), bf16)], axis=0)
        scaled = scaled_ref[slot]
        expected = jnp.dot(scaled, recv_pad, preferred_element_type=f32)
        ratios = (counts[slot].astype(f32) * live / expected).astype(bf16)
        toward_send = lax.dot_general(
            ratios, recv_pad, (((1,), (1,)), ((), ())), preferred_element_type=f32
        )
        toward_recv = jnp.dot(turned_ref[slot], ratios, preferred_element_type=f32)
        send_term = scaled.astype(f32) * toward_send
        recv_term = recv.astype(f32) * toward_recv
        return send_term, recv_term, jnp.sum(send_term, axis=0, keepdims=True)

    def one_group(group, carry):
        done = [one_tile(group * unroll + u) for u in range(unroll)]
        for u, (send_term, recv_term, act_term) in enumerate(done):
            slot = group * unroll + u
            send_slots[slot] = send_term + send_slots[prev[0, slot]]
            recv_slots[slot] = recv_term + recv_slots[prev[1, slot]]
            act_rows[pl.ds(slot, 1), :] = act_term
        return carry

    lax.fori_loop(0, slots // unroll, one_group, 0)

    action_id = lax.broadcasted_iota(jnp.int32, (actions, slots), 0)
    onehot = jnp.where(action_id == aid_row[...], 1.0, 0.0).astype(f32)
    act_sum = jnp.dot(
        onehot, act_rows[...], preferred_element_type=f32, precision=lax.Precision.HIGHEST
    )
    for chunk in range(n_rcv):
        act_own[chunk, :act_chunk] = act_sum[chunk * act_chunk : (chunk + 1) * act_chunk].astype(
            bf16
        )
    acts = Group((pair_sems.at[1, 0], pair_sems.at[1, 1]))
    for o in range(1, n_rcv):
        other = lax.rem(rcv + o, n_rcv)
        acts.start(act_own.at[other], act_dst.at[rcv], {"rcv": other})
    act_dst[rcv] = act_own[rcv]

    def hand_over(block, carry):
        value = recv_slots[last_recv[block]].astype(bf16)
        begin = block * span
        ty, tz = begin // side, lax.rem(begin, side)
        for e in range(span):
            columns = value[:, e * lanes : (e + 1) * lanes]
            parts[0, ty, slot_at(tz + e - z, side)] = columns[:rows]
            parts[1, tz + e, slot_at(ty - y, side)] = columns[rows:]
        return carry

    lax.fori_loop(0, blocks, hand_over, 0, unroll=2)

    def piece_of(kind, distance, start, size):
        return parts.at[kind, block_at(kind, distance), pl.ds(start, size)]

    out_ring = [Group((ring_send.at[1, kind], None)) for kind in (0, 1)]
    backwards = tuple(reversed(range(len(pieces))))

    def far_parts(index):
        start, size = pieces[index]
        for kind in (0, 1):
            for way in (0, 1):
                sign = 1 - 2 * way
                at = (kind, way, pl.ds(start, size))
                arrive = ring_recv.at[1, kind, way, index]
                if (start < half) == (way == 0):
                    out_ring[kind].start(
                        piece_of(kind, 4 * sign, start, size),
                        from4.at[at],
                        to_ring(kind, 2 * sign),
                        arrive,
                    )
                out_ring[kind].start(
                    piece_of(kind, 3 * sign, start, size), from3.at[at], to_ring(kind, sign), arrive
                )

    def join(index):
        start, size = pieces[index]
        for kind in (0, 1):
            for way in (0, 1):
                sign = 1 - 2 * way
                at = (kind, way, pl.ds(start, size))
                both = (start < half) == (way == 0)
                settle(
                    ring_recv.at[1, kind, way, index],
                    parts.at[0, 0, pl.ds(0, size * (2 if both else 1))],
                )
                total = parts[kind, block_at(kind, 2 * sign), pl.ds(start, size)].astype(f32)
                total = total + from3[at].astype(f32)
                if both:
                    total = total + from4[at].astype(f32)
                joined[at] = total.astype(bf16)
                out_ring[kind].start(
                    joined.at[at], from2.at[at], to_ring(kind, 2 * sign), done_recv.at[kind, index]
                )
        for kind in (0, 1):
            for way in (0, 1):
                sign = 1 - 2 * way
                out_ring[kind].start(
                    piece_of(kind, sign, start, size),
                    from1.at[kind, way, pl.ds(start, size)],
                    to_ring(kind, sign),
                    done_recv.at[kind, index],
                )

    def total_of(ref, count):
        value = ref[0].astype(f32)
        for index in range(1, count):
            value = value + ref[index].astype(f32)
        return value

    def spread(level, value):
        me = where[level]
        sum_src[level] = value.astype(bf16)
        sum_dst[level, me] = value.astype(bf16)
        group = Group((pair_sems.at[2 + level, 0], pair_sems.at[2 + level, 1]))
        for o in far_first(side):
            group.start(sum_src.at[level], sum_dst.at[level, me], to_ring(level, o))

    def split_totals(value):
        tail = value[act_chunk:]
        result = jnp.zeros_like(tail)
        for base in (0, 3):
            row = tail[base : base + 1] + (tail[base + 1 : base + 2] + tail[base + 2 : base + 3])
            for index, part in enumerate(split3(row)):
                result = jnp.where(row_id == base + index, part, result)
        return jnp.concatenate([value[:act_chunk], result], axis=0)

    last = [Group((last_sems.at[kind, 0], last_sems.at[kind, 1])) for kind in (0, 1)]

    def finish(index):
        start, size = pieces[index]
        for kind in (0, 1):
            settle(done_recv.at[kind, index], parts.at[0, pl.ds(0, size), pl.ds(0, 4)])
            total = parts[kind, where[kind], pl.ds(start, size)].astype(f32)
            for way in (0, 1):
                at = (kind, way, pl.ds(start, size))
                total = total + from1[at].astype(f32) + from2[at].astype(f32)
            near_src[kind, pl.ds(start, size)] = total.astype(bf16)
            for offset in far_first(side):
                slot = slot_of(offset, side)
                if start <= slot < start + size:
                    last[kind].start(
                        near_src.at[kind, slot],
                        near_dst.at[kind, slot_of(side - offset, side)],
                        near_peer[kind](y, z, side, offset),
                    )

    for index in backwards:
        far_parts(index)

    def give(block, carry):
        value = send_slots[last_send[block]].astype(bf16)
        for e in range(span):
            send_part[block * span + e] = value[e * lanes : (e + 1) * lanes]
        return carry

    lax.fori_loop(0, send_blocks, give, 0)
    sends = Group((pair_sems.at[4, 0], pair_sems.at[4, 1]))
    for o in range(1, n_rcv):
        other = lax.rem(rcv + o, n_rcv)
        sends.start(send_part.at[other], send_dst.at[rcv], {"rcv": other})
    send_dst[rcv] = send_part[rcv]

    settle(pair_sems.at[1, 1], act_dst.at[pl.ds(0, n_rcv - 1)])
    spread(0, split_totals(total_of(act_dst, n_rcv)))
    for index in backwards:
        join(index)
    settle(pair_sems.at[2, 1], sum_dst.at[0, pl.ds(0, side - 1)])
    spread(1, split_totals(total_of(sum_dst.at[0], side)))
    for index in backwards:
        finish(index)
    for kind in (0, 1):
        near_dst[kind, 0] = near_src[kind, 0]
    settle(pair_sems.at[3, 1], sum_dst.at[1, pl.ds(0, side - 1)])
    full = total_of(sum_dst.at[1], side)
    act_out[pl.ds(rcv * act_chunk, act_chunk), :] = full[:act_chunk]
    own = act_out.at[pl.ds(rcv * act_chunk, act_chunk), :]
    back = Group((pair_sems.at[5, 0], pair_sems.at[5, 1]))
    for o in range(1, n_rcv):
        back.start(own, own, peer_r(rcv, n_rcv, o))
    tot_out[...] = full[act_chunk:]
    settle(pair_sems.at[4, 1], send_dst.at[pl.ds(0, n_rcv - 1)])
    send_out[...] = total_of(send_dst, n_rcv)

    for kind in (0, 1):
        settle(near_sems.at[kind, 0], refs[kind].at[0, pl.ds(0, side - 1)])
        settle(ring_send.at[0, kind], refs[kind].at[pl.ds(0, side - 1)])
        settle(ring_send.at[1, kind], refs[kind].at[pl.ds(0, side - 1)])
    settle(pair_sems.at[0, 0], sgeo_ref.at[pl.ds(0, n_rcv - 1)])
    settle(pair_sems.at[1, 0], act_dst.at[pl.ds(0, n_rcv - 1)])
    settle(pair_sems.at[2, 0], sum_dst.at[0, pl.ds(0, side - 1)])
    settle(pair_sems.at[3, 0], sum_dst.at[1, pl.ds(0, side - 1)])
    settle(pair_sems.at[4, 0], send_dst.at[pl.ds(0, n_rcv - 1)])
    for kind in (0, 1):
        settle(last_sems.at[kind, 1], near_dst.at[kind, pl.ds(0, side - 1)])
        recv_out[kind * rows : (kind + 1) * rows] = total_of(near_dst.at[kind], side)
    for kind in (0, 1):
        settle(last_sems.at[kind, 0], near_dst.at[kind, pl.ds(0, side - 1)])
    for end in (1, 0):
        settle(pair_sems.at[5, end], act_out.at[pl.ds(0, (n_rcv - 1) * act_chunk), :])


def refresh_kernel(*refs):
    sources, outs, refs = refs[:10], refs[10:16], refs[16:]
    held, load_sem = refs[:10], refs[10]
    for index in range(10):
        pltpu.make_async_copy(sources[index], held[index], load_sem.at[index]).start()
    for index in range(10):
        pltpu.make_async_copy(sources[index], held[index], load_sem.at[index]).wait()
    ss_ref, sr_ref, rs_ref, rr_ref, as_ref, ar_ref, send_ref, recv_ref, act_ref, tot_ref = held
    ss_out, sr_out, rs_out, rr_out, as_out, ar_out = outs
    rank = as_ref.shape[0]
    row = lax.broadcasted_iota(jnp.int32, (rank, lanes), 0)
    col = lax.broadcasted_iota(jnp.int32, (rank, lanes), 1)

    def column(index):
        parts = [tot_ref[pl.ds(index + part, 1), :] for part in range(3)]
        wide = jnp.broadcast_to(parts[0] + (parts[1] + parts[2]), (rank, lanes))
        return jnp.sum(jnp.where(row == col, wide, 0.0), axis=1, keepdims=True)

    send_total, recv_total = column(0), column(3)
    act_total = jnp.sum(jnp.exp(as_ref[...] - ar_ref[...]), axis=1, keepdims=True)
    ss_out[0] = refresh(ss_ref[0], prior_shape + send_ref[...].T[:rank])
    sr_out[0] = refresh(sr_ref[0], prior_rate + recv_total * act_total)
    rs_out[0] = refresh(rs_ref[0], prior_shape + recv_ref[...])
    rr_out[0] = refresh(rr_ref[0], prior_rate + send_total * act_total)
    as_out[...] = refresh(as_ref[...], prior_shape + act_ref[...].T[:rank])
    ar_out[...] = refresh(ar_ref[...], prior_rate + send_total * recv_total)


def per_device(
    side,
    n_rcv,
    tile_counts,
    tile_sender,
    tile_receiver,
    tile_action,
    tile_fill,
    ss,
    sr,
    rs,
    rr,
    ash,
    art,
):
    rank, actions = ash.shape
    slots, edge = tile_counts.shape[2], tile_counts.shape[3]
    rows, span = rank // 2, edge // lanes
    blocks, send_blocks = side * side // span, n_rcv // span
    vmem = pl.BlockSpec(memory_space=pltpu.VMEM)
    hbm = pl.BlockSpec(memory_space=pltpu.HBM)
    shape = jax.ShapeDtypeStruct
    dma = pltpu.SemaphoreType.DMA
    geo = pltpu.VMEM((side, side, rows, lanes), bf16)
    landing = pltpu.VMEM((2, 2, side, rows, lanes), bf16)
    near = pltpu.VMEM((2, side, rows, lanes), bf16)
    sender = pltpu.VMEM((n_rcv, lanes, lanes), bf16)
    chunk = actions // n_rcv + 16

    recv_stat, send_stat, act_stat, totals = pl.pallas_call(
        functools.partial(fused_kernel, side, n_rcv),
        out_shape=(
            shape((rank, lanes), f32),
            shape((lanes, lanes), f32),
            shape((actions, lanes), f32),
            shape((16, lanes), f32),
        ),
        in_specs=[hbm] * 11,
        out_specs=(vmem,) * 4,
        scratch_shapes=[
            pltpu.VMEM((4, rank, lanes), f32),
            pltpu.VMEM((2, rank, actions), f32),
            pltpu.SMEM((3, 1, slots), jnp.int32),
            pltpu.SMEM(tile_fill.shape, jnp.int32),
            pltpu.VMEM((1, slots), jnp.int32),
            pltpu.SMEM((2, slots), jnp.int32),
            pltpu.SMEM((blocks,), jnp.int32),
            pltpu.SMEM((send_blocks,), jnp.int32),
            pltpu.VMEM((slots, edge, edge), bf16),
            geo,
            geo,
            sender,
            pltpu.VMEM((actions, lanes), f32),
            pltpu.VMEM((slots, edge, lanes), bf16),
            pltpu.VMEM((slots, rank, edge), bf16),
            pltpu.VMEM((slots + 1, edge, lanes), f32),
            pltpu.VMEM((slots + 1, rank, edge), f32),
            pltpu.VMEM((slots, lanes), f32),
            pltpu.VMEM((2, side, side, rows, lanes), bf16),
            landing,
            landing,
            landing,
            landing,
            landing,
            near,
            near,
            sender,
            sender,
            pltpu.VMEM((n_rcv, chunk, lanes), bf16),
            pltpu.VMEM((n_rcv, chunk, lanes), bf16),
            pltpu.VMEM((2, chunk, lanes), bf16),
            pltpu.VMEM((2, side, chunk, lanes), bf16),
            dma((6,)),
            dma((2, 3)),
            dma((2, 2)),
            dma((2, 2, 2, 3)),
            dma((2,)),
            dma((2, 3)),
            dma((2, 2)),
            dma((6, 2)),
        ],
        compiler_params=pltpu.CompilerParams(
            collective_id=0, has_side_effects=True, vmem_limit_bytes=whole_vmem
        ),
    )(
        tile_counts,
        tile_sender,
        tile_receiver,
        tile_action,
        tile_fill,
        ss,
        sr,
        rs,
        rr,
        ash,
        art,
    )

    sources = (ss, sr, rs, rr, ash, art, send_stat, recv_stat, act_stat, totals)
    return pl.pallas_call(
        refresh_kernel,
        out_shape=tuple(shape(x.shape, f32) for x in (ss, sr, rs, rr, ash, art)),
        in_specs=[hbm] * len(sources),
        out_specs=(vmem,) * 6,
        scratch_shapes=[pltpu.VMEM(x.shape, f32) for x in sources] + [dma((len(sources),))],
        compiler_params=pltpu.CompilerParams(vmem_limit_bytes=whole_vmem),
    )(*sources)


def solution(mesh):
    n_snd, n_rcv = mesh.shape["snd"], mesh.shape["rcv"]
    side = round(n_snd**0.5)
    return jax.shard_map(
        functools.partial(per_device, side, n_rcv),
        mesh=mesh,
        in_specs=(
            P("snd", "rcv", None, None, None),
            P("snd", "rcv", None),
            P("snd", "rcv", None),
            P("snd", "rcv", None),
            P("snd", "rcv"),
            P("snd", None, "rcv"),
            P("snd", None, "rcv"),
            P("rcv", None, "snd"),
            P("rcv", None, "snd"),
            P(),
            P(),
        ),
        out_specs=(
            P("snd", None, "rcv"),
            P("snd", None, "rcv"),
            P("rcv", None, "snd"),
            P("rcv", None, "snd"),
            P(),
            P(),
        ),
        check_vma=False,
    )
```

```python
import functools

import jax
import jax.numpy as jnp
from jax import lax
from jax.experimental import pallas as pl
from jax.experimental.pallas import tpu as pltpu
from jax.sharding import PartitionSpec as P

prior_shape = 0.3
prior_rate = 0.3
step_size = 0.5
lanes = 128
unroll = 8
whole_vmem = 60 << 20

MESH = pl.DeviceIdType.MESH
bf16 = jnp.bfloat16
f32 = jnp.float32


def digamma_series(value):
    shift_sum = jnp.zeros_like(value)
    for offset in range(6):
        shift_sum = shift_sum + 1.0 / (value + float(offset))
    moved = value + 6.0
    inverse = 1.0 / moved
    inv_square = inverse * inverse
    series = (
        jnp.log(moved)
        - 0.5 * inverse
        - inv_square * (1.0 / 12.0 - inv_square * (1.0 / 120.0 - inv_square / 252.0))
    )
    return series - shift_sum


def geometric(log_shape, log_rate):
    return jnp.exp(digamma_series(jnp.exp(log_shape)) - log_rate)


def refresh(log_value, target):
    return jnp.log((1.0 - step_size) * jnp.exp(log_value) + step_size * target)


def turned(value):
    rank, cols = value.shape
    padded = jnp.concatenate([value, jnp.zeros((lanes - rank, cols), value.dtype)], axis=0)
    return padded.T


def place(side):
    snd = lax.axis_index("snd")
    return snd // side, lax.rem(snd, side), lax.axis_index("rcv")


def peer_y(y, z, side, offset):
    return {"snd": lax.rem(y + offset + side, side) * side + z}


def peer_z(y, z, side, offset):
    return {"snd": y * side + lax.rem(z + offset + side, side)}


def peer_r(rcv, n_rcv, offset):
    return {"rcv": lax.rem(rcv + offset, n_rcv)}


def greet(side, n_rcv):
    y, z, rcv = place(side)
    barrier = pltpu.get_barrier_semaphore()
    for offset in far_first(side):
        for peer in (peer_y, peer_z):
            pl.semaphore_signal(
                barrier, inc=1, device_id=peer(y, z, side, offset), device_id_type=MESH
            )
    for offset in range(1, n_rcv):
        pl.semaphore_signal(
            barrier, inc=1, device_id=peer_r(rcv, n_rcv, offset), device_id_type=MESH
        )
    return barrier, 2 * (side - 1) + n_rcv - 1


def far_first(side):
    return sorted(range(1, side), key=lambda o: -min(o, side - o))


def slot_of(offset, side):
    return 0 if offset == 0 else (2 * offset - 1 if offset <= side // 2 else 2 * (side - offset))


def slot_at(offset, side):
    offset = lax.rem(offset + side, side)
    near = jnp.maximum(2 * offset - 1, 0)
    return jnp.where(offset <= side // 2, near, 2 * (side - offset))


class Group:
    def __init__(self, sems):
        self.sems = sems

    def start(self, src, dst, device, arrive=None):
        pltpu.make_async_remote_copy(
            src_ref=src,
            dst_ref=dst,
            send_sem=self.sems[0],
            recv_sem=arrive if arrive is not None else self.sems[1],
            device_id=device,
            device_id_type=MESH,
        ).start()


def settle(sem, like):
    pltpu.make_async_copy(like, like, sem).wait()


def fused_kernel(
    side,
    n_rcv,
    counts_hbm,
    sid_hbm,
    rid_hbm,
    aid_hbm,
    fill_hbm,
    ss_hbm,
    sr_hbm,
    rs_hbm,
    rr_hbm,
    as_hbm,
    ar_hbm,
    recv_out,
    send_out,
    act_out,
    tot_out,
    own_ref,
    act_ref,
    ids,
    fill,
    aid_row,
    prev,
    last_recv,
    last_send,
    counts,
    top_ref,
    low_ref,
    sgeo_ref,
    ageo_ref,
    scaled_ref,
    turned_ref,
    send_slots,
    recv_slots,
    act_rows,
    parts,
    from1,
    from2,
    from3,
    from4,
    joined,
    near_src,
    near_dst,
    send_part,
    send_dst,
    act_own,
    act_dst,
    sum_src,
    sum_dst,
    tot_src,
    tot_dst,
    load_sem,
    near_sems,
    ring_send,
    ring_recv,
    rest_recv,
    done_recv,
    last_sems,
    pair_sems,
    tot_sems,
):
    y, z, rcv = place(side)
    half = side // 2
    slots, edge = counts.shape[0], counts.shape[1]
    span = edge // lanes
    rank, rows = own_ref.shape[1], top_ref.shape[2]
    actions = ageo_ref.shape[0]
    blocks, send_blocks = side * side // span, n_rcv // span

    loads = [
        pltpu.make_async_copy(src, dst, load_sem.at[index])
        for index, src, dst in (
            (0, rs_hbm.at[0], own_ref.at[0]),
            (0, rr_hbm.at[0], own_ref.at[1]),
            (0, ss_hbm.at[0], own_ref.at[2]),
            (0, sr_hbm.at[0], own_ref.at[3]),
            (1, as_hbm, act_ref.at[0]),
            (1, ar_hbm, act_ref.at[1]),
            (2, sid_hbm.at[0], ids.at[0]),
            (2, rid_hbm.at[0], ids.at[1]),
            (2, aid_hbm.at[0], ids.at[2]),
            (3, fill_hbm, fill),
            (4, aid_hbm.at[0], aid_row),
            (5, counts_hbm.at[0, 0], counts),
        )
    ]
    for copy in loads:
        copy.start()
    barrier, greeted = greet(side, n_rcv)
    settle(load_sem.at[0], own_ref)
    geo = geometric(own_ref[0], own_ref[1]).astype(bf16)
    top_ref[y, 0] = geo[:rows]
    low_ref[z, 0] = geo[rows:]
    sgeo_ref[rcv] = turned(geometric(own_ref[2], own_ref[3])).astype(bf16)
    pl.semaphore_wait(barrier, greeted)

    refs, where = (top_ref, low_ref), (y, z)
    ring_peer, near_peer = (peer_y, peer_z), (peer_z, peer_y)
    pieces = ((0, 1), (1, half - 1), (half, side - half))

    def to_ring(kind, distance):
        return ring_peer[kind](y, z, side, distance)

    def block_at(kind, distance):
        return lax.rem(where[kind] + distance + side, side)

    near = [Group((near_sems.at[kind, 0], None)) for kind in (0, 1)]
    ring = [Group((ring_send.at[0, kind], rest_recv.at[kind])) for kind in (0, 1)]

    def forward(index):
        start, size = pieces[index]
        for kind in (0, 1):
            part = refs[kind].at[where[kind], pl.ds(start, size)]
            if start:
                settle(near_sems.at[kind, index], part)
            for way in (0, 1):
                ring[kind].start(
                    part, part, to_ring(kind, 2 - 4 * way), ring_recv.at[0, kind, way, index]
                )

    def onward(index):
        start, size = pieces[index]
        for kind in (0, 1):
            for way in (0, 1):
                sign = 1 - 2 * way
                part = refs[kind].at[block_at(kind, -2 * sign), pl.ds(start, size)]
                settle(ring_recv.at[0, kind, way, index], part)
                if (start < half) == (way == 0):
                    ring[kind].start(part, part, to_ring(kind, 2 * sign))
                ring[kind].start(part, part, to_ring(kind, sign))

    for offset in far_first(side):
        for kind in (0, 1):
            slot = slot_of(side - offset, side)
            near[kind].start(
                refs[kind].at[where[kind], 0],
                refs[kind].at[where[kind], slot],
                near_peer[kind](y, z, side, offset),
                near_sems.at[kind, 1 if slot < half else 2],
            )
    forward(0)
    across = Group((pair_sems.at[0, 0], pair_sems.at[0, 1]))
    for o in range(1, n_rcv):
        across.start(sgeo_ref.at[rcv], sgeo_ref.at[rcv], peer_r(rcv, n_rcv, o))

    settle(load_sem.at[1], act_ref)
    settle(load_sem.at[2], ids)
    ageo_ref[...] = turned(geometric(act_ref[0], act_ref[1]))

    send_row = jnp.sum(turned(jnp.exp(own_ref[2] - own_ref[3])), axis=0, keepdims=True)
    recv_row = jnp.sum(turned(jnp.exp(own_ref[0] - own_ref[1])), axis=0, keepdims=True)
    tot_src[0, 0:1] = send_row
    tot_src[0, 1:2] = recv_row

    def totals_in(level):
        settle(tot_sems.at[level, 1], tot_dst.at[level, pl.ds(0, (n_rcv, side, side)[level] - 1)])
        value = tot_dst[level, 0]
        for index in range(1, (n_rcv, side, side)[level]):
            value = value + tot_dst[level, index]
        return value

    def exchange_totals(level):
        if level:
            tot_src[level] = totals_in(level - 1)
        me = (rcv, y, z)[level]
        tot_dst[level, me] = tot_src[level]
        group = Group((tot_sems.at[level, 0], tot_sems.at[level, 1]))
        for o in range(1, (n_rcv, side, side)[level]):
            device = peer_r(rcv, n_rcv, o) if level == 0 else to_ring(level - 1, o)
            group.start(tot_src.at[level], tot_dst.at[level, me], device)

    def link(slot, carry):
        b, c = ids[0, 0, slot], ids[1, 0, slot]
        before_b, before_c = jnp.int32(slots), jnp.int32(slots)
        for other in range(slots):
            earlier = other < slot
            before_b = jnp.where((ids[0, 0, other] == b) & earlier, other, before_b)
            before_c = jnp.where((ids[1, 0, other] == c) & earlier, other, before_c)
        prev[0, slot] = before_b
        prev[1, slot] = before_c
        return carry

    def final(row, table):
        def body(block, carry):
            found = jnp.int32(slots)
            for other in range(slots):
                found = jnp.where(ids[row, 0, other] == block, other, found)
            table[block] = found
            return carry

        return body

    exchange_totals(0)
    lax.fori_loop(0, slots, link, 0)
    for index in range(1, len(pieces)):
        forward(index)
    exchange_totals(1)
    for index in range(len(pieces)):
        onward(index)
    for kind in (0, 1):
        part = refs[kind].at[where[kind]]
        for sign in (1, -1):
            ring[kind].start(part, part, to_ring(kind, sign))

    exchange_totals(2)
    settle(pair_sems.at[0, 1], sgeo_ref.at[pl.ds(0, n_rcv - 1)])

    def scale(slot, carry):
        b, a = ids[0, 0, slot], ids[2, 0, slot]
        sender = sgeo_ref[pl.ds(b * span, span)].reshape(edge, lanes)
        scaled = (sender.astype(f32) * ageo_ref[pl.ds(a, 1), :]).astype(bf16)
        scaled_ref[slot] = scaled
        turned_ref[slot] = scaled.T[:rank]
        return carry

    lax.fori_loop(0, slots, scale, 0, unroll=4)
    lax.fori_loop(0, blocks, final(1, last_recv), 0)
    lax.fori_loop(0, send_blocks, final(0, last_send), 0)
    act_chunk = actions // n_rcv
    send_slots[slots] = jnp.zeros(send_slots.shape[1:], f32)
    recv_slots[slots] = jnp.zeros(recv_slots.shape[1:], f32)
    settle(load_sem.at[3], fill)
    settle(load_sem.at[4], aid_row)
    settle(load_sem.at[5], counts)
    for kind in (0, 1):
        settle(rest_recv.at[kind], refs[kind].at[pl.ds(0, 5)])

    live_count = fill[0, 0]

    def recv_block(slot):
        begin = ids[1, 0, slot] * span
        ty, tz = begin // side, lax.rem(begin, side)
        down = slot_at(ty - y, side)
        return jnp.concatenate(
            [
                jnp.concatenate(
                    [top_ref[ty, slot_at(tz + e - z, side)] for e in range(span)], axis=1
                ),
                jnp.concatenate([low_ref[tz + e, down] for e in range(span)], axis=1),
            ],
            axis=0,
        )

    def padded(recv):
        return jnp.concatenate([recv, jnp.zeros((lanes - rank, edge), bf16)], axis=0)

    def ratio_tile(slot):
        live = jnp.where(slot < live_count, 1.0, 0.0).astype(f32)
        expected = jnp.dot(
            scaled_ref[slot], padded(recv_block(slot)), preferred_element_type=f32
        )
        return (counts[slot].astype(f32) * live / expected).astype(bf16)

    def ratio_group(group, carry):
        done = [ratio_tile(group * unroll + u) for u in range(unroll)]
        for u, ratios in enumerate(done):
            counts[group * unroll + u] = ratios
        return carry

    lax.fori_loop(0, slots // unroll, ratio_group, 0)

    def stat_tile(slot):
        recv, scaled, ratios = recv_block(slot), scaled_ref[slot], counts[slot]
        toward_send = lax.dot_general(
            ratios, padded(recv), (((1,), (1,)), ((), ())), preferred_element_type=f32
        )
        toward_recv = jnp.dot(turned_ref[slot], ratios, preferred_element_type=f32)
        send_term = scaled.astype(f32) * toward_send
        recv_term = recv.astype(f32) * toward_recv
        return send_term, recv_term, jnp.sum(send_term, axis=0, keepdims=True)

    def stat_group(group, carry):
        done = [stat_tile(group * unroll + u) for u in range(unroll)]
        for u, (send_term, recv_term, act_term) in enumerate(done):
            slot = group * unroll + u
            send_slots[slot] = send_term + send_slots[prev[0, slot]]
            recv_slots[slot] = recv_term + recv_slots[prev[1, slot]]
            act_rows[pl.ds(slot, 1), :] = act_term
        return carry

    lax.fori_loop(0, slots // unroll, stat_group, 0)

    action_id = lax.broadcasted_iota(jnp.int32, (actions, slots), 0)
    onehot = jnp.where(action_id == aid_row[...], 1.0, 0.0).astype(f32)
    act_sum = jnp.dot(
        onehot, act_rows[...], preferred_element_type=f32, precision=lax.Precision.HIGHEST
    )
    for chunk in range(n_rcv):
        act_own[chunk] = act_sum[chunk * act_chunk : (chunk + 1) * act_chunk].astype(bf16)
    acts = Group((pair_sems.at[1, 0], pair_sems.at[1, 1]))
    for o in range(1, n_rcv):
        other = lax.rem(rcv + o, n_rcv)
        acts.start(act_own.at[other], act_dst.at[rcv], {"rcv": other})
    act_dst[rcv] = act_own[rcv]

    def hand_over(kind, distance):
        line = block_at(kind, distance)
        if kind == 0:
            for block in range(side // span):
                table = last_recv[line * (side // span) + block]
                value = recv_slots[table, pl.ds(0, rows), :].astype(bf16)
                for e in range(span):
                    slot = slot_at(block * span + e - z, side)
                    parts[0, line, slot] = value[:, e * lanes : (e + 1) * lanes]
        else:
            block = line // span
            column = pl.multiple_of(lax.rem(line, span) * lanes, lanes)
            for ty in range(side):
                table = last_recv[ty * (side // span) + block]
                value = recv_slots[table, pl.ds(rows, rows), pl.ds(column, lanes)]
                parts[1, line, slot_at(ty - y, side)] = value.astype(bf16)

    def piece_of(kind, distance, start, size):
        return parts.at[kind, block_at(kind, distance), pl.ds(start, size)]

    out_ring = [Group((ring_send.at[1, kind], None)) for kind in (0, 1)]
    backwards = tuple(reversed(range(len(pieces))))

    def far_parts(index):
        start, size = pieces[index]
        for kind in (0, 1):
            for way in (0, 1):
                sign = 1 - 2 * way
                at = (kind, way, pl.ds(start, size))
                arrive = ring_recv.at[1, kind, way, index]
                if (start < half) == (way == 0):
                    out_ring[kind].start(
                        piece_of(kind, 4 * sign, start, size),
                        from4.at[at],
                        to_ring(kind, 2 * sign),
                        arrive,
                    )
                out_ring[kind].start(
                    piece_of(kind, 3 * sign, start, size), from3.at[at], to_ring(kind, sign), arrive
                )

    def join(index):
        start, size = pieces[index]
        for kind in (0, 1):
            for way in (0, 1):
                sign = 1 - 2 * way
                at = (kind, way, pl.ds(start, size))
                both = (start < half) == (way == 0)
                settle(
                    ring_recv.at[1, kind, way, index],
                    parts.at[0, 0, pl.ds(0, size * (2 if both else 1))],
                )
                total = parts[kind, block_at(kind, 2 * sign), pl.ds(start, size)].astype(f32)
                total = total + from3[at].astype(f32)
                if both:
                    total = total + from4[at].astype(f32)
                joined[at] = total.astype(bf16)
                out_ring[kind].start(
                    joined.at[at], from2.at[at], to_ring(kind, 2 * sign), done_recv.at[kind, index]
                )
        for kind in (0, 1):
            for way in (0, 1):
                sign = 1 - 2 * way
                out_ring[kind].start(
                    piece_of(kind, sign, start, size),
                    from1.at[kind, way, pl.ds(start, size)],
                    to_ring(kind, sign),
                    done_recv.at[kind, index],
                )

    def total_of(ref, count):
        value = ref[0].astype(f32)
        for index in range(1, count):
            value = value + ref[index].astype(f32)
        return value

    def spread(level, value):
        me = where[level]
        sum_src[level] = value.astype(bf16)
        sum_dst[level, me] = value.astype(bf16)
        group = Group((pair_sems.at[2 + level, 0], pair_sems.at[2 + level, 1]))
        for o in far_first(side):
            group.start(sum_src.at[level], sum_dst.at[level, me], to_ring(level, o))

    last = [Group((last_sems.at[kind, 0], last_sems.at[kind, 1])) for kind in (0, 1)]

    def finish(index):
        start, size = pieces[index]
        for kind in (0, 1):
            settle(done_recv.at[kind, index], parts.at[0, pl.ds(0, size), pl.ds(0, 4)])
            total = parts[kind, where[kind], pl.ds(start, size)].astype(f32)
            for way in (0, 1):
                at = (kind, way, pl.ds(start, size))
                total = total + from1[at].astype(f32) + from2[at].astype(f32)
            near_src[kind, pl.ds(start, size)] = total.astype(bf16)
            for offset in far_first(side):
                slot = slot_of(offset, side)
                if start <= slot < start + size:
                    last[kind].start(
                        near_src.at[kind, slot],
                        near_dst.at[kind, slot_of(side - offset, side)],
                        near_peer[kind](y, z, side, offset),
                    )

    for distance in (half, half - 1, 1 - half):
        for kind in (0, 1):
            hand_over(kind, distance)
    for index in backwards:
        far_parts(index)
    for distance in (2, -2, 1, -1, 0):
        for kind in (0, 1):
            hand_over(kind, distance)

    def give(block, carry):
        value = send_slots[last_send[block]].astype(bf16)
        for e in range(span):
            send_part[block * span + e] = value[e * lanes : (e + 1) * lanes]
        return carry

    lax.fori_loop(0, send_blocks, give, 0)
    sends = Group((pair_sems.at[4, 0], pair_sems.at[4, 1]))
    for o in range(1, n_rcv):
        other = lax.rem(rcv + o, n_rcv)
        sends.start(send_part.at[other], send_dst.at[rcv], {"rcv": other})
    send_dst[rcv] = send_part[rcv]

    settle(pair_sems.at[1, 1], act_dst.at[pl.ds(0, n_rcv - 1)])
    spread(0, total_of(act_dst, n_rcv))
    for index in backwards:
        join(index)
    settle(pair_sems.at[2, 1], sum_dst.at[0, pl.ds(0, side - 1)])
    spread(1, total_of(sum_dst.at[0], side))
    for index in backwards:
        finish(index)
    for kind in (0, 1):
        near_dst[kind, 0] = near_src[kind, 0]
    settle(pair_sems.at[3, 1], sum_dst.at[1, pl.ds(0, side - 1)])
    act_out[pl.ds(rcv * act_chunk, act_chunk), :] = total_of(sum_dst.at[1], side)
    own = act_out.at[pl.ds(rcv * act_chunk, act_chunk), :]
    back = Group((pair_sems.at[5, 0], pair_sems.at[5, 1]))
    for o in range(1, n_rcv):
        back.start(own, own, peer_r(rcv, n_rcv, o))
    tot_out[...] = totals_in(2)
    settle(pair_sems.at[4, 1], send_dst.at[pl.ds(0, n_rcv - 1)])
    send_out[...] = total_of(send_dst, n_rcv)

    for kind in (0, 1):
        settle(near_sems.at[kind, 0], refs[kind].at[0, pl.ds(0, side - 1)])
        settle(ring_send.at[0, kind], refs[kind].at[pl.ds(0, side - 1)])
        settle(ring_send.at[1, kind], refs[kind].at[pl.ds(0, side - 1)])
    for level in range(3):
        like = tot_dst.at[level, pl.ds(0, (n_rcv, side, side)[level] - 1)]
        settle(tot_sems.at[level, 0], like)
    settle(pair_sems.at[0, 0], sgeo_ref.at[pl.ds(0, n_rcv - 1)])
    settle(pair_sems.at[1, 0], act_dst.at[pl.ds(0, n_rcv - 1)])
    settle(pair_sems.at[2, 0], sum_dst.at[0, pl.ds(0, side - 1)])
    settle(pair_sems.at[3, 0], sum_dst.at[1, pl.ds(0, side - 1)])
    settle(pair_sems.at[4, 0], send_dst.at[pl.ds(0, n_rcv - 1)])
    for kind in (0, 1):
        settle(last_sems.at[kind, 1], near_dst.at[kind, pl.ds(0, side - 1)])
        recv_out[kind * rows : (kind + 1) * rows] = total_of(near_dst.at[kind], side)
    for kind in (0, 1):
        settle(last_sems.at[kind, 0], near_dst.at[kind, pl.ds(0, side - 1)])
    for end in (1, 0):
        settle(pair_sems.at[5, end], act_out.at[pl.ds(0, (n_rcv - 1) * act_chunk), :])


def refresh_kernel(*refs):
    sources, outs, refs = refs[:10], refs[10:16], refs[16:]
    held, load_sem = refs[:10], refs[10]
    for index in range(10):
        pltpu.make_async_copy(sources[index], held[index], load_sem.at[index]).start()
    for index in range(10):
        pltpu.make_async_copy(sources[index], held[index], load_sem.at[index]).wait()
    ss_ref, sr_ref, rs_ref, rr_ref, as_ref, ar_ref, send_ref, recv_ref, act_ref, tot_ref = held
    ss_out, sr_out, rs_out, rr_out, as_out, ar_out = outs
    rank = as_ref.shape[0]
    row = lax.broadcasted_iota(jnp.int32, (rank, lanes), 0)
    col = lax.broadcasted_iota(jnp.int32, (rank, lanes), 1)

    def column(index):
        wide = jnp.broadcast_to(tot_ref[pl.ds(index, 1), :], (rank, lanes))
        return jnp.sum(jnp.where(row == col, wide, 0.0), axis=1, keepdims=True)

    send_total, recv_total = column(0), column(1)
    act_total = jnp.sum(jnp.exp(as_ref[...] - ar_ref[...]), axis=1, keepdims=True)
    ss_out[0] = refresh(ss_ref[0], prior_shape + send_ref[...].T[:rank])
    sr_out[0] = refresh(sr_ref[0], prior_rate + recv_total * act_total)
    rs_out[0] = refresh(rs_ref[0], prior_shape + recv_ref[...])
    rr_out[0] = refresh(rr_ref[0], prior_rate + send_total * act_total)
    as_out[...] = refresh(as_ref[...], prior_shape + act_ref[...].T[:rank])
    ar_out[...] = refresh(ar_ref[...], prior_rate + send_total * recv_total)


def per_device(
    side,
    n_rcv,
    tile_counts,
    tile_sender,
    tile_receiver,
    tile_action,
    tile_fill,
    ss,
    sr,
    rs,
    rr,
    ash,
    art,
):
    rank, actions = ash.shape
    slots, edge = tile_counts.shape[2], tile_counts.shape[3]
    rows, span = rank // 2, edge // lanes
    blocks, send_blocks = side * side // span, n_rcv // span
    vmem = pl.BlockSpec(memory_space=pltpu.VMEM)
    hbm = pl.BlockSpec(memory_space=pltpu.HBM)
    shape = jax.ShapeDtypeStruct
    dma = pltpu.SemaphoreType.DMA
    geo = pltpu.VMEM((side, side, rows, lanes), bf16)
    landing = pltpu.VMEM((2, 2, side, rows, lanes), bf16)
    near = pltpu.VMEM((2, side, rows, lanes), bf16)
    sender = pltpu.VMEM((n_rcv, lanes, lanes), bf16)
    chunk = actions // n_rcv

    recv_stat, send_stat, act_stat, totals = pl.pallas_call(
        functools.partial(fused_kernel, side, n_rcv),
        out_shape=(
            shape((rank, lanes), f32),
            shape((lanes, lanes), f32),
            shape((actions, lanes), f32),
            shape((2, lanes), f32),
        ),
        in_specs=[hbm] * 11,
        out_specs=(vmem,) * 4,
        scratch_shapes=[
            pltpu.VMEM((4, rank, lanes), f32),
            pltpu.VMEM((2, rank, actions), f32),
            pltpu.SMEM((3, 1, slots), jnp.int32),
            pltpu.SMEM(tile_fill.shape, jnp.int32),
            pltpu.VMEM((1, slots), jnp.int32),
            pltpu.SMEM((2, slots), jnp.int32),
            pltpu.SMEM((blocks,), jnp.int32),
            pltpu.SMEM((send_blocks,), jnp.int32),
            pltpu.VMEM((slots, edge, edge), bf16),
            geo,
            geo,
            sender,
            pltpu.VMEM((actions, lanes), f32),
            pltpu.VMEM((slots, edge, lanes), bf16),
            pltpu.VMEM((slots, rank, edge), bf16),
            pltpu.VMEM((slots + 1, edge, lanes), f32),
            pltpu.VMEM((slots + 1, rank, edge), f32),
            pltpu.VMEM((slots, lanes), f32),
            pltpu.VMEM((2, side, side, rows, lanes), bf16),
            landing,
            landing,
            landing,
            landing,
            landing,
            near,
            near,
            sender,
            sender,
            pltpu.VMEM((n_rcv, chunk, lanes), bf16),
            pltpu.VMEM((n_rcv, chunk, lanes), bf16),
            pltpu.VMEM((2, chunk, lanes), bf16),
            pltpu.VMEM((2, side, chunk, lanes), bf16),
            pltpu.VMEM((3, 2, lanes), f32),
            pltpu.VMEM((3, max(side, n_rcv), 2, lanes), f32),
            dma((6,)),
            dma((2, 3)),
            dma((2, 2)),
            dma((2, 2, 2, 3)),
            dma((2,)),
            dma((2, 3)),
            dma((2, 2)),
            dma((6, 2)),
            dma((3, 2)),
        ],
        compiler_params=pltpu.CompilerParams(
            collective_id=0, has_side_effects=True, vmem_limit_bytes=whole_vmem
        ),
    )(
        tile_counts,
        tile_sender,
        tile_receiver,
        tile_action,
        tile_fill,
        ss,
        sr,
        rs,
        rr,
        ash,
        art,
    )

    sources = (ss, sr, rs, rr, ash, art, send_stat, recv_stat, act_stat, totals)
    return pl.pallas_call(
        refresh_kernel,
        out_shape=tuple(shape(x.shape, f32) for x in (ss, sr, rs, rr, ash, art)),
        in_specs=[hbm] * len(sources),
        out_specs=(vmem,) * 6,
        scratch_shapes=[pltpu.VMEM(x.shape, f32) for x in sources] + [dma((len(sources),))],
        compiler_params=pltpu.CompilerParams(vmem_limit_bytes=whole_vmem),
    )(*sources)


def solution(mesh):
    n_snd, n_rcv = mesh.shape["snd"], mesh.shape["rcv"]
    side = round(n_snd**0.5)
    return jax.shard_map(
        functools.partial(per_device, side, n_rcv),
        mesh=mesh,
        in_specs=(
            P("snd", "rcv", None, None, None),
            P("snd", "rcv", None),
            P("snd", "rcv", None),
            P("snd", "rcv", None),
            P("snd", "rcv"),
            P("snd", None, "rcv"),
            P("snd", None, "rcv"),
            P("rcv", None, "snd"),
            P("rcv", None, "snd"),
            P(),
            P(),
        ),
        out_specs=(
            P("snd", None, "rcv"),
            P("snd", None, "rcv"),
            P("rcv", None, "snd"),
            P("rcv", None, "snd"),
            P(),
            P(),
        ),
        check_vma=False,
    )
```

```python
import functools

import jax
import jax.numpy as jnp
from jax import lax
from jax.experimental import pallas as pl
from jax.experimental.pallas import tpu as pltpu
from jax.sharding import PartitionSpec as P

prior_shape = 0.3
prior_rate = 0.3
step_size = 0.5
lanes = 128
unroll = 8
whole_vmem = 60 << 20

MESH = pl.DeviceIdType.MESH
bf16 = jnp.bfloat16
f32 = jnp.float32


def digamma_series(value):
    shift_sum = jnp.zeros_like(value)
    for offset in range(6):
        shift_sum = shift_sum + 1.0 / (value + float(offset))
    moved = value + 6.0
    inverse = 1.0 / moved
    inv_square = inverse * inverse
    series = (
        jnp.log(moved)
        - 0.5 * inverse
        - inv_square * (1.0 / 12.0 - inv_square * (1.0 / 120.0 - inv_square / 252.0))
    )
    return series - shift_sum


def geometric(log_shape, log_rate):
    return jnp.exp(digamma_series(jnp.exp(log_shape)) - log_rate)


def refresh(log_value, target):
    return jnp.log((1.0 - step_size) * jnp.exp(log_value) + step_size * target)


def turned(value):
    rank, cols = value.shape
    padded = jnp.concatenate([value, jnp.zeros((lanes - rank, cols), value.dtype)], axis=0)
    return padded.T


def place(side):
    snd = lax.axis_index("snd")
    return snd // side, lax.rem(snd, side), lax.axis_index("rcv")


def peer_y(y, z, side, offset):
    return {"snd": lax.rem(y + offset + side, side) * side + z}


def peer_z(y, z, side, offset):
    return {"snd": y * side + lax.rem(z + offset + side, side)}


def peer_r(rcv, n_rcv, offset):
    return {"rcv": lax.rem(rcv + offset, n_rcv)}


def greet(side, n_rcv):
    y, z, rcv = place(side)
    barrier = pltpu.get_barrier_semaphore()
    for offset in far_first(side):
        for peer in (peer_y, peer_z):
            pl.semaphore_signal(
                barrier, inc=1, device_id=peer(y, z, side, offset), device_id_type=MESH
            )
    for offset in range(1, n_rcv):
        pl.semaphore_signal(
            barrier, inc=1, device_id=peer_r(rcv, n_rcv, offset), device_id_type=MESH
        )
    return barrier, 2 * (side - 1) + n_rcv - 1


def far_first(side):
    return sorted(range(1, side), key=lambda o: -min(o, side - o))


def slot_of(offset, side):
    return 0 if offset == 0 else (2 * offset - 1 if offset <= side // 2 else 2 * (side - offset))


def slot_at(offset, side):
    offset = lax.rem(offset + side, side)
    near = jnp.maximum(2 * offset - 1, 0)
    return jnp.where(offset <= side // 2, near, 2 * (side - offset))


class Group:
    def __init__(self, sems):
        self.sems = sems

    def start(self, src, dst, device, arrive=None):
        pltpu.make_async_remote_copy(
            src_ref=src,
            dst_ref=dst,
            send_sem=self.sems[0],
            recv_sem=arrive if arrive is not None else self.sems[1],
            device_id=device,
            device_id_type=MESH,
        ).start()


def settle(sem, like):
    pltpu.make_async_copy(like, like, sem).wait()


def fused_kernel(
    side,
    n_rcv,
    counts_hbm,
    sid_hbm,
    rid_hbm,
    aid_hbm,
    fill_hbm,
    ss_hbm,
    sr_hbm,
    rs_hbm,
    rr_hbm,
    as_hbm,
    ar_hbm,
    recv_out,
    send_out,
    act_out,
    tot_out,
    own_ref,
    act_ref,
    ids,
    fill,
    aid_row,
    prev,
    last_recv,
    last_send,
    counts,
    top_ref,
    low_ref,
    sgeo_ref,
    ageo_ref,
    scaled_ref,
    turned_ref,
    send_slots,
    recv_slots,
    act_rows,
    parts,
    from1,
    from2,
    from3,
    from4,
    joined,
    near_src,
    near_dst,
    send_part,
    send_dst,
    act_own,
    act_dst,
    sum_src,
    sum_dst,
    tot_src,
    tot_dst,
    load_sem,
    near_sems,
    ring_send,
    ring_recv,
    rest_recv,
    done_recv,
    last_sems,
    pair_sems,
    tot_sems,
):
    y, z, rcv = place(side)
    half = side // 2
    slots, edge = counts.shape[0], counts.shape[1]
    span = edge // lanes
    rank, rows = own_ref.shape[1], top_ref.shape[2]
    actions = ageo_ref.shape[0]
    blocks, send_blocks = side * side // span, n_rcv // span

    loads = [
        pltpu.make_async_copy(src, dst, load_sem.at[index])
        for index, src, dst in (
            (0, rs_hbm.at[0], own_ref.at[0]),
            (0, rr_hbm.at[0], own_ref.at[1]),
            (0, ss_hbm.at[0], own_ref.at[2]),
            (0, sr_hbm.at[0], own_ref.at[3]),
            (1, as_hbm, act_ref.at[0]),
            (1, ar_hbm, act_ref.at[1]),
            (2, sid_hbm.at[0], ids.at[0]),
            (2, rid_hbm.at[0], ids.at[1]),
            (2, aid_hbm.at[0], ids.at[2]),
            (3, fill_hbm, fill),
            (4, aid_hbm.at[0], aid_row),
            (5, counts_hbm.at[0, 0], counts),
        )
    ]
    for copy in loads:
        copy.start()
    barrier, greeted = greet(side, n_rcv)
    settle(load_sem.at[0], own_ref)
    geo = geometric(own_ref[0], own_ref[1]).astype(bf16)
    top_ref[y, 0] = geo[:rows]
    low_ref[z, 0] = geo[rows:]
    sgeo_ref[rcv] = turned(geometric(own_ref[2], own_ref[3])).astype(bf16)
    pl.semaphore_wait(barrier, greeted)

    refs, where = (top_ref, low_ref), (y, z)
    ring_peer, near_peer = (peer_y, peer_z), (peer_z, peer_y)
    pieces = ((0, 1), (1, half - 1), (half, side - half))

    def to_ring(kind, distance):
        return ring_peer[kind](y, z, side, distance)

    def block_at(kind, distance):
        return lax.rem(where[kind] + distance + side, side)

    near = [Group((near_sems.at[kind, 0], None)) for kind in (0, 1)]
    ring = [Group((ring_send.at[0, kind], rest_recv.at[kind])) for kind in (0, 1)]

    def forward(index):
        start, size = pieces[index]
        for kind in (0, 1):
            part = refs[kind].at[where[kind], pl.ds(start, size)]
            if start:
                settle(near_sems.at[kind, index], part)
            for way in (0, 1):
                ring[kind].start(
                    part, part, to_ring(kind, 2 - 4 * way), ring_recv.at[0, kind, way, index]
                )

    def onward(index):
        start, size = pieces[index]
        for kind in (0, 1):
            for way in (0, 1):
                sign = 1 - 2 * way
                part = refs[kind].at[block_at(kind, -2 * sign), pl.ds(start, size)]
                settle(ring_recv.at[0, kind, way, index], part)
                if (start < half) == (way == 0):
                    ring[kind].start(part, part, to_ring(kind, 2 * sign))
                ring[kind].start(part, part, to_ring(kind, sign))

    for offset in far_first(side):
        for kind in (0, 1):
            slot = slot_of(side - offset, side)
            near[kind].start(
                refs[kind].at[where[kind], 0],
                refs[kind].at[where[kind], slot],
                near_peer[kind](y, z, side, offset),
                near_sems.at[kind, 1 if slot < half else 2],
            )
    forward(0)
    across = Group((pair_sems.at[0, 0], pair_sems.at[0, 1]))
    for o in range(1, n_rcv):
        across.start(sgeo_ref.at[rcv], sgeo_ref.at[rcv], peer_r(rcv, n_rcv, o))

    settle(load_sem.at[1], act_ref)
    settle(load_sem.at[2], ids)
    ageo_ref[...] = turned(geometric(act_ref[0], act_ref[1]))

    send_row = jnp.sum(turned(jnp.exp(own_ref[2] - own_ref[3])), axis=0, keepdims=True)
    recv_row = jnp.sum(turned(jnp.exp(own_ref[0] - own_ref[1])), axis=0, keepdims=True)
    tot_src[0, 0:1] = send_row
    tot_src[0, 1:2] = recv_row

    def totals_in(level):
        settle(tot_sems.at[level, 1], tot_dst.at[level, pl.ds(0, (n_rcv, side, side)[level] - 1)])
        value = tot_dst[level, 0]
        for index in range(1, (n_rcv, side, side)[level]):
            value = value + tot_dst[level, index]
        return value

    def exchange_totals(level):
        if level:
            tot_src[level] = totals_in(level - 1)
        me = (rcv, y, z)[level]
        tot_dst[level, me] = tot_src[level]
        group = Group((tot_sems.at[level, 0], tot_sems.at[level, 1]))
        for o in range(1, (n_rcv, side, side)[level]):
            device = peer_r(rcv, n_rcv, o) if level == 0 else to_ring(level - 1, o)
            group.start(tot_src.at[level], tot_dst.at[level, me], device)

    def link(slot, carry):
        b, c = ids[0, 0, slot], ids[1, 0, slot]
        before_b, before_c = jnp.int32(slots), jnp.int32(slots)
        for other in range(slots):
            earlier = other < slot
            before_b = jnp.where((ids[0, 0, other] == b) & earlier, other, before_b)
            before_c = jnp.where((ids[1, 0, other] == c) & earlier, other, before_c)
        prev[0, slot] = before_b
        prev[1, slot] = before_c
        return carry

    def final(row, table):
        def body(block, carry):
            found = jnp.int32(slots)
            for other in range(slots):
                found = jnp.where(ids[row, 0, other] == block, other, found)
            table[block] = found
            return carry

        return body

    exchange_totals(0)
    lax.fori_loop(0, slots, link, 0)
    for index in range(1, len(pieces)):
        forward(index)
    exchange_totals(1)
    for index in range(len(pieces)):
        onward(index)
    for kind in (0, 1):
        part = refs[kind].at[where[kind]]
        for sign in (1, -1):
            ring[kind].start(part, part, to_ring(kind, sign))

    exchange_totals(2)
    settle(pair_sems.at[0, 1], sgeo_ref.at[pl.ds(0, n_rcv - 1)])

    def scale(slot, carry):
        b, a = ids[0, 0, slot], ids[2, 0, slot]
        sender = sgeo_ref[pl.ds(b * span, span)].reshape(edge, lanes)
        scaled = (sender.astype(f32) * ageo_ref[pl.ds(a, 1), :]).astype(bf16)
        scaled_ref[slot] = scaled
        turned_ref[slot] = scaled.T[:rank]
        return carry

    lax.fori_loop(0, slots, scale, 0, unroll=4)
    lax.fori_loop(0, blocks, final(1, last_recv), 0)
    lax.fori_loop(0, send_blocks, final(0, last_send), 0)
    act_chunk = actions // n_rcv
    send_slots[slots] = jnp.zeros(send_slots.shape[1:], f32)
    recv_slots[slots] = jnp.zeros(recv_slots.shape[1:], f32)
    settle(load_sem.at[3], fill)
    settle(load_sem.at[4], aid_row)
    settle(load_sem.at[5], counts)
    for kind in (0, 1):
        settle(rest_recv.at[kind], refs[kind].at[pl.ds(0, 5)])

    live_count = fill[0, 0]

    def recv_block(slot):
        begin = ids[1, 0, slot] * span
        ty, tz = begin // side, lax.rem(begin, side)
        down = slot_at(ty - y, side)
        return jnp.concatenate(
            [
                jnp.concatenate(
                    [top_ref[ty, slot_at(tz + e - z, side)] for e in range(span)], axis=1
                ),
                jnp.concatenate([low_ref[tz + e, down] for e in range(span)], axis=1),
            ],
            axis=0,
        )

    def padded(recv):
        return jnp.concatenate([recv, jnp.zeros((lanes - rank, edge), bf16)], axis=0)

    def ratio_tile(slot):
        live = jnp.where(slot < live_count, 1.0, 0.0).astype(f32)
        expected = jnp.dot(
            scaled_ref[slot], padded(recv_block(slot)), preferred_element_type=f32
        )
        return (counts[slot].astype(f32) * live / expected).astype(bf16)

    def ratio_group(group, carry):
        done = [ratio_tile(group * unroll + u) for u in range(unroll)]
        for u, ratios in enumerate(done):
            counts[group * unroll + u] = ratios
        return carry

    lax.fori_loop(0, slots // unroll, ratio_group, 0)

    def stat_tile(slot):
        recv, scaled, ratios = recv_block(slot), scaled_ref[slot], counts[slot]
        toward_send = lax.dot_general(
            ratios, padded(recv), (((1,), (1,)), ((), ())), preferred_element_type=f32
        )
        toward_recv = jnp.dot(turned_ref[slot], ratios, preferred_element_type=f32)
        send_term = scaled.astype(f32) * toward_send
        recv_term = recv.astype(f32) * toward_recv
        return send_term, recv_term, jnp.sum(send_term, axis=0, keepdims=True)

    def stat_group(group, carry):
        done = [stat_tile(group * unroll + u) for u in range(unroll)]
        for u, (send_term, recv_term, act_term) in enumerate(done):
            slot = group * unroll + u
            send_slots[slot] = send_term + send_slots[prev[0, slot]]
            recv_slots[slot] = recv_term + recv_slots[prev[1, slot]]
            act_rows[pl.ds(slot, 1), :] = act_term
        return carry

    lax.fori_loop(0, slots // unroll, stat_group, 0)

    action_id = lax.broadcasted_iota(jnp.int32, (actions, slots), 0)
    onehot = jnp.where(action_id == aid_row[...], 1.0, 0.0).astype(f32)
    act_sum = jnp.dot(
        onehot, act_rows[...], preferred_element_type=f32, precision=lax.Precision.HIGHEST
    )
    for chunk in range(n_rcv):
        act_own[chunk] = act_sum[chunk * act_chunk : (chunk + 1) * act_chunk].astype(bf16)
    acts = Group((pair_sems.at[1, 0], pair_sems.at[1, 1]))
    for o in range(1, n_rcv):
        other = lax.rem(rcv + o, n_rcv)
        acts.start(act_own.at[other], act_dst.at[rcv], {"rcv": other})
    act_dst[rcv] = act_own[rcv]

    def hand_over(kind, distance):
        line = block_at(kind, distance)
        if kind == 0:
            for block in range(side // span):
                table = last_recv[line * (side // span) + block]
                value = recv_slots[table, pl.ds(0, rows), :].astype(bf16)
                for e in range(span):
                    slot = slot_at(block * span + e - z, side)
                    parts[0, line, slot] = value[:, e * lanes : (e + 1) * lanes]
        else:
            block = line // span
            column = pl.multiple_of(lax.rem(line, span) * lanes, lanes)
            for ty in range(side):
                table = last_recv[ty * (side // span) + block]
                value = recv_slots[table, pl.ds(rows, rows), pl.ds(column, lanes)]
                parts[1, line, slot_at(ty - y, side)] = value.astype(bf16)

    def piece_of(kind, distance, start, size):
        return parts.at[kind, block_at(kind, distance), pl.ds(start, size)]

    out_ring = [Group((ring_send.at[1, kind], None)) for kind in (0, 1)]
    backwards = tuple(reversed(range(len(pieces))))

    def far_parts(index):
        start, size = pieces[index]
        for kind in (0, 1):
            for way in (0, 1):
                sign = 1 - 2 * way
                at = (kind, way, pl.ds(start, size))
                arrive = ring_recv.at[1, kind, way, index]
                if (start < half) == (way == 0):
                    out_ring[kind].start(
                        piece_of(kind, 4 * sign, start, size),
                        from4.at[at],
                        to_ring(kind, 2 * sign),
                        arrive,
                    )
                out_ring[kind].start(
                    piece_of(kind, 3 * sign, start, size), from3.at[at], to_ring(kind, sign), arrive
                )

    def join(index):
        start, size = pieces[index]
        for kind in (0, 1):
            for way in (0, 1):
                sign = 1 - 2 * way
                at = (kind, way, pl.ds(start, size))
                both = (start < half) == (way == 0)
                settle(
                    ring_recv.at[1, kind, way, index],
                    parts.at[0, 0, pl.ds(0, size * (2 if both else 1))],
                )
                total = parts[kind, block_at(kind, 2 * sign), pl.ds(start, size)].astype(f32)
                total = total + from3[at].astype(f32)
                if both:
                    total = total + from4[at].astype(f32)
                joined[at] = total.astype(bf16)
                out_ring[kind].start(
                    joined.at[at], from2.at[at], to_ring(kind, 2 * sign), done_recv.at[kind, index]
                )
        for kind in (0, 1):
            for way in (0, 1):
                sign = 1 - 2 * way
                out_ring[kind].start(
                    piece_of(kind, sign, start, size),
                    from1.at[kind, way, pl.ds(start, size)],
                    to_ring(kind, sign),
                    done_recv.at[kind, index],
                )

    def total_of(ref, count):
        value = ref[0].astype(f32)
        for index in range(1, count):
            value = value + ref[index].astype(f32)
        return value

    def spread(level, value):
        me = where[level]
        sum_src[level] = value.astype(bf16)
        sum_dst[level, me] = value.astype(bf16)
        group = Group((pair_sems.at[2 + level, 0], pair_sems.at[2 + level, 1]))
        for o in far_first(side):
            group.start(sum_src.at[level], sum_dst.at[level, me], to_ring(level, o))

    last = [Group((last_sems.at[kind, 0], last_sems.at[kind, 1])) for kind in (0, 1)]

    def finish(index):
        start, size = pieces[index]
        for kind in (0, 1):
            settle(done_recv.at[kind, index], parts.at[0, pl.ds(0, size), pl.ds(0, 4)])
            total = parts[kind, where[kind], pl.ds(start, size)].astype(f32)
            for way in (0, 1):
                at = (kind, way, pl.ds(start, size))
                total = total + from1[at].astype(f32) + from2[at].astype(f32)
            near_src[kind, pl.ds(start, size)] = total.astype(bf16)
            for offset in far_first(side):
                slot = slot_of(offset, side)
                if start <= slot < start + size:
                    last[kind].start(
                        near_src.at[kind, slot],
                        near_dst.at[kind, slot_of(side - offset, side)],
                        near_peer[kind](y, z, side, offset),
                    )

    for distance in (half, half - 1, 1 - half):
        for kind in (0, 1):
            hand_over(kind, distance)
    for index in backwards:
        far_parts(index)
    for distance in (2, -2, 1, -1, 0):
        for kind in (0, 1):
            hand_over(kind, distance)

    def give(block, carry):
        value = send_slots[last_send[block]].astype(bf16)
        for e in range(span):
            send_part[block * span + e] = value[e * lanes : (e + 1) * lanes]
        return carry

    lax.fori_loop(0, send_blocks, give, 0)
    sends = Group((pair_sems.at[4, 0], pair_sems.at[4, 1]))
    for o in range(1, n_rcv):
        other = lax.rem(rcv + o, n_rcv)
        sends.start(send_part.at[other], send_dst.at[rcv], {"rcv": other})
    send_dst[rcv] = send_part[rcv]

    settle(pair_sems.at[1, 1], act_dst.at[pl.ds(0, n_rcv - 1)])
    spread(0, total_of(act_dst, n_rcv))
    join(backwards[0])
    join(backwards[1])
    settle(pair_sems.at[2, 1], sum_dst.at[0, pl.ds(0, side - 1)])
    spread(1, total_of(sum_dst.at[0], side))
    join(backwards[2])
    finish(backwards[0])
    finish(backwards[1])
    settle(pair_sems.at[3, 1], sum_dst.at[1, pl.ds(0, side - 1)])
    act_out[pl.ds(rcv * act_chunk, act_chunk), :] = total_of(sum_dst.at[1], side)
    own = act_out.at[pl.ds(rcv * act_chunk, act_chunk), :]
    back = Group((pair_sems.at[5, 0], pair_sems.at[5, 1]))
    for o in range(1, n_rcv):
        back.start(own, own, peer_r(rcv, n_rcv, o))
    finish(backwards[2])
    for kind in (0, 1):
        near_dst[kind, 0] = near_src[kind, 0]
    tot_out[...] = totals_in(2)
    settle(pair_sems.at[4, 1], send_dst.at[pl.ds(0, n_rcv - 1)])
    send_out[...] = total_of(send_dst, n_rcv)

    for kind in (0, 1):
        settle(near_sems.at[kind, 0], refs[kind].at[0, pl.ds(0, side - 1)])
        settle(ring_send.at[0, kind], refs[kind].at[pl.ds(0, side - 1)])
        settle(ring_send.at[1, kind], refs[kind].at[pl.ds(0, side - 1)])
    for level in range(3):
        like = tot_dst.at[level, pl.ds(0, (n_rcv, side, side)[level] - 1)]
        settle(tot_sems.at[level, 0], like)
    settle(pair_sems.at[0, 0], sgeo_ref.at[pl.ds(0, n_rcv - 1)])
    settle(pair_sems.at[1, 0], act_dst.at[pl.ds(0, n_rcv - 1)])
    settle(pair_sems.at[2, 0], sum_dst.at[0, pl.ds(0, side - 1)])
    settle(pair_sems.at[3, 0], sum_dst.at[1, pl.ds(0, side - 1)])
    settle(pair_sems.at[4, 0], send_dst.at[pl.ds(0, n_rcv - 1)])
    for kind in (0, 1):
        settle(last_sems.at[kind, 1], near_dst.at[kind, pl.ds(0, side - 1)])
        recv_out[kind * rows : (kind + 1) * rows] = total_of(near_dst.at[kind], side)
    for kind in (0, 1):
        settle(last_sems.at[kind, 0], near_dst.at[kind, pl.ds(0, side - 1)])
    for end in (1, 0):
        settle(pair_sems.at[5, end], act_out.at[pl.ds(0, (n_rcv - 1) * act_chunk), :])


def refresh_kernel(*refs):
    sources, outs, refs = refs[:10], refs[10:16], refs[16:]
    held, load_sem = refs[:10], refs[10]
    for index in range(10):
        pltpu.make_async_copy(sources[index], held[index], load_sem.at[index]).start()
    for index in range(10):
        pltpu.make_async_copy(sources[index], held[index], load_sem.at[index]).wait()
    ss_ref, sr_ref, rs_ref, rr_ref, as_ref, ar_ref, send_ref, recv_ref, act_ref, tot_ref = held
    ss_out, sr_out, rs_out, rr_out, as_out, ar_out = outs
    rank = as_ref.shape[0]
    row = lax.broadcasted_iota(jnp.int32, (rank, lanes), 0)
    col = lax.broadcasted_iota(jnp.int32, (rank, lanes), 1)

    def column(index):
        wide = jnp.broadcast_to(tot_ref[pl.ds(index, 1), :], (rank, lanes))
        return jnp.sum(jnp.where(row == col, wide, 0.0), axis=1, keepdims=True)

    send_total, recv_total = column(0), column(1)
    act_total = jnp.sum(jnp.exp(as_ref[...] - ar_ref[...]), axis=1, keepdims=True)
    ss_out[0] = refresh(ss_ref[0], prior_shape + send_ref[...].T[:rank])
    sr_out[0] = refresh(sr_ref[0], prior_rate + recv_total * act_total)
    rs_out[0] = refresh(rs_ref[0], prior_shape + recv_ref[...])
    rr_out[0] = refresh(rr_ref[0], prior_rate + send_total * act_total)
    as_out[...] = refresh(as_ref[...], prior_shape + act_ref[...].T[:rank])
    ar_out[...] = refresh(ar_ref[...], prior_rate + send_total * recv_total)


def per_device(
    side,
    n_rcv,
    tile_counts,
    tile_sender,
    tile_receiver,
    tile_action,
    tile_fill,
    ss,
    sr,
    rs,
    rr,
    ash,
    art,
):
    rank, actions = ash.shape
    slots, edge = tile_counts.shape[2], tile_counts.shape[3]
    rows, span = rank // 2, edge // lanes
    blocks, send_blocks = side * side // span, n_rcv // span
    vmem = pl.BlockSpec(memory_space=pltpu.VMEM)
    hbm = pl.BlockSpec(memory_space=pltpu.HBM)
    shape = jax.ShapeDtypeStruct
    dma = pltpu.SemaphoreType.DMA
    geo = pltpu.VMEM((side, side, rows, lanes), bf16)
    landing = pltpu.VMEM((2, 2, side, rows, lanes), bf16)
    near = pltpu.VMEM((2, side, rows, lanes), bf16)
    sender = pltpu.VMEM((n_rcv, lanes, lanes), bf16)
    chunk = actions // n_rcv

    recv_stat, send_stat, act_stat, totals = pl.pallas_call(
        functools.partial(fused_kernel, side, n_rcv),
        out_shape=(
            shape((rank, lanes), f32),
            shape((lanes, lanes), f32),
            shape((actions, lanes), f32),
            shape((2, lanes), f32),
        ),
        in_specs=[hbm] * 11,
        out_specs=(vmem,) * 4,
        scratch_shapes=[
            pltpu.VMEM((4, rank, lanes), f32),
            pltpu.VMEM((2, rank, actions), f32),
            pltpu.SMEM((3, 1, slots), jnp.int32),
            pltpu.SMEM(tile_fill.shape, jnp.int32),
            pltpu.VMEM((1, slots), jnp.int32),
            pltpu.SMEM((2, slots), jnp.int32),
            pltpu.SMEM((blocks,), jnp.int32),
            pltpu.SMEM((send_blocks,), jnp.int32),
            pltpu.VMEM((slots, edge, edge), bf16),
            geo,
            geo,
            sender,
            pltpu.VMEM((actions, lanes), f32),
            pltpu.VMEM((slots, edge, lanes), bf16),
            pltpu.VMEM((slots, rank, edge), bf16),
            pltpu.VMEM((slots + 1, edge, lanes), f32),
            pltpu.VMEM((slots + 1, rank, edge), f32),
            pltpu.VMEM((slots, lanes), f32),
            pltpu.VMEM((2, side, side, rows, lanes), bf16),
            landing,
            landing,
            landing,
            landing,
            landing,
            near,
            near,
            sender,
            sender,
            pltpu.VMEM((n_rcv, chunk, lanes), bf16),
            pltpu.VMEM((n_rcv, chunk, lanes), bf16),
            pltpu.VMEM((2, chunk, lanes), bf16),
            pltpu.VMEM((2, side, chunk, lanes), bf16),
            pltpu.VMEM((3, 2, lanes), f32),
            pltpu.VMEM((3, max(side, n_rcv), 2, lanes), f32),
            dma((6,)),
            dma((2, 3)),
            dma((2, 2)),
            dma((2, 2, 2, 3)),
            dma((2,)),
            dma((2, 3)),
            dma((2, 2)),
            dma((6, 2)),
            dma((3, 2)),
        ],
        compiler_params=pltpu.CompilerParams(
            collective_id=0, has_side_effects=True, vmem_limit_bytes=whole_vmem
        ),
    )(
        tile_counts,
        tile_sender,
        tile_receiver,
        tile_action,
        tile_fill,
        ss,
        sr,
        rs,
        rr,
        ash,
        art,
    )

    sources = (ss, sr, rs, rr, ash, art, send_stat, recv_stat, act_stat, totals)
    return pl.pallas_call(
        refresh_kernel,
        out_shape=tuple(shape(x.shape, f32) for x in (ss, sr, rs, rr, ash, art)),
        in_specs=[hbm] * len(sources),
        out_specs=(vmem,) * 6,
        scratch_shapes=[pltpu.VMEM(x.shape, f32) for x in sources] + [dma((len(sources),))],
        compiler_params=pltpu.CompilerParams(vmem_limit_bytes=whole_vmem),
    )(*sources)


def solution(mesh):
    n_snd, n_rcv = mesh.shape["snd"], mesh.shape["rcv"]
    side = round(n_snd**0.5)
    return jax.shard_map(
        functools.partial(per_device, side, n_rcv),
        mesh=mesh,
        in_specs=(
            P("snd", "rcv", None, None, None),
            P("snd", "rcv", None),
            P("snd", "rcv", None),
            P("snd", "rcv", None),
            P("snd", "rcv"),
            P("snd", None, "rcv"),
            P("snd", None, "rcv"),
            P("rcv", None, "snd"),
            P("rcv", None, "snd"),
            P(),
            P(),
        ),
        out_specs=(
            P("snd", None, "rcv"),
            P("snd", None, "rcv"),
            P("rcv", None, "snd"),
            P("rcv", None, "snd"),
            P(),
            P(),
        ),
        check_vma=False,
    )
```

```python
import functools

import jax
import jax.numpy as jnp
from jax import lax
from jax.experimental import pallas as pl
from jax.experimental.pallas import tpu as pltpu
from jax.sharding import PartitionSpec as P

prior_shape = 0.3
prior_rate = 0.3
step_size = 0.5
lanes = 128
unroll = 8
whole_vmem = 60 << 20

MESH = pl.DeviceIdType.MESH
bf16 = jnp.bfloat16
f32 = jnp.float32


def digamma_series(value):
    shift_sum = jnp.zeros_like(value)
    for offset in range(6):
        shift_sum = shift_sum + 1.0 / (value + float(offset))
    moved = value + 6.0
    inverse = 1.0 / moved
    inv_square = inverse * inverse
    series = (
        jnp.log(moved)
        - 0.5 * inverse
        - inv_square * (1.0 / 12.0 - inv_square * (1.0 / 120.0 - inv_square / 252.0))
    )
    return series - shift_sum


def geometric(log_shape, log_rate):
    return jnp.exp(digamma_series(jnp.exp(log_shape)) - log_rate)


def refresh(log_value, target):
    return jnp.log((1.0 - step_size) * jnp.exp(log_value) + step_size * target)


def turned(value):
    rank, cols = value.shape
    padded = jnp.concatenate([value, jnp.zeros((lanes - rank, cols), value.dtype)], axis=0)
    return padded.T


def place(side):
    snd = lax.axis_index("snd")
    return snd // side, lax.rem(snd, side), lax.axis_index("rcv")


def peer_y(y, z, side, offset):
    return {"snd": lax.rem(y + offset + side, side) * side + z}


def peer_z(y, z, side, offset):
    return {"snd": y * side + lax.rem(z + offset + side, side)}


def peer_r(rcv, n_rcv, offset):
    return {"rcv": lax.rem(rcv + offset, n_rcv)}


def greet(side, n_rcv):
    y, z, rcv = place(side)
    barrier = pltpu.get_barrier_semaphore()
    for offset in far_first(side):
        for peer in (peer_y, peer_z):
            pl.semaphore_signal(
                barrier, inc=1, device_id=peer(y, z, side, offset), device_id_type=MESH
            )
    for offset in range(1, n_rcv):
        pl.semaphore_signal(
            barrier, inc=1, device_id=peer_r(rcv, n_rcv, offset), device_id_type=MESH
        )
    return barrier, 2 * (side - 1) + n_rcv - 1


def far_first(side):
    return sorted(range(1, side), key=lambda o: -min(o, side - o))


def slot_of(offset, side):
    return 0 if offset == 0 else (2 * offset - 1 if offset <= side // 2 else 2 * (side - offset))


def slot_at(offset, side):
    offset = lax.rem(offset + side, side)
    near = jnp.maximum(2 * offset - 1, 0)
    return jnp.where(offset <= side // 2, near, 2 * (side - offset))


class Group:
    def __init__(self, sems):
        self.sems = sems

    def start(self, src, dst, device, arrive=None):
        pltpu.make_async_remote_copy(
            src_ref=src,
            dst_ref=dst,
            send_sem=self.sems[0],
            recv_sem=arrive if arrive is not None else self.sems[1],
            device_id=device,
            device_id_type=MESH,
        ).start()


def settle(sem, like):
    pltpu.make_async_copy(like, like, sem).wait()


def fused_kernel(
    side,
    n_rcv,
    counts_hbm,
    sid_hbm,
    rid_hbm,
    aid_hbm,
    fill_hbm,
    ss_hbm,
    sr_hbm,
    rs_hbm,
    rr_hbm,
    as_hbm,
    ar_hbm,
    recv_out,
    send_out,
    act_out,
    tot_out,
    own_ref,
    act_ref,
    ids,
    fill,
    aid_row,
    prev,
    last_recv,
    last_send,
    counts,
    top_ref,
    low_ref,
    sgeo_ref,
    ageo_ref,
    scaled_ref,
    turned_ref,
    send_slots,
    recv_slots,
    act_rows,
    parts,
    from1,
    from2,
    from3,
    from4,
    joined,
    near_src,
    near_dst,
    send_part,
    send_dst,
    act_own,
    act_dst,
    sum_src,
    sum_dst,
    tot_src,
    tot_dst,
    load_sem,
    near_sems,
    ring_send,
    ring_recv,
    rest_recv,
    done_recv,
    last_sems,
    pair_sems,
    tot_sems,
):
    y, z, rcv = place(side)
    half = side // 2
    slots, edge = counts.shape[0], counts.shape[1]
    span = edge // lanes
    rank, rows = own_ref.shape[1], top_ref.shape[2]
    actions = ageo_ref.shape[0]
    blocks, send_blocks = side * side // span, n_rcv // span

    loads = [
        pltpu.make_async_copy(src, dst, load_sem.at[index])
        for index, src, dst in (
            (0, rs_hbm.at[0], own_ref.at[0]),
            (0, rr_hbm.at[0], own_ref.at[1]),
            (0, ss_hbm.at[0], own_ref.at[2]),
            (0, sr_hbm.at[0], own_ref.at[3]),
            (1, as_hbm, act_ref.at[0]),
            (1, ar_hbm, act_ref.at[1]),
            (2, sid_hbm.at[0], ids.at[0]),
            (2, rid_hbm.at[0], ids.at[1]),
            (2, aid_hbm.at[0], ids.at[2]),
            (3, fill_hbm, fill),
            (4, aid_hbm.at[0], aid_row),
            (5, counts_hbm.at[0, 0], counts),
        )
    ]
    for copy in loads:
        copy.start()
    barrier, greeted = greet(side, n_rcv)
    settle(load_sem.at[0], own_ref)
    geo = geometric(own_ref[0], own_ref[1]).astype(bf16)
    top_ref[y, 0] = geo[:rows]
    low_ref[z, 0] = geo[rows:]
    sgeo_ref[rcv] = turned(geometric(own_ref[2], own_ref[3])).astype(bf16)
    pl.semaphore_wait(barrier, greeted)

    refs, where = (top_ref, low_ref), (y, z)
    ring_peer, near_peer = (peer_y, peer_z), (peer_z, peer_y)
    pieces = ((0, 1), (1, half - 1), (half, side - half))

    def to_ring(kind, distance):
        return ring_peer[kind](y, z, side, distance)

    def block_at(kind, distance):
        return lax.rem(where[kind] + distance + side, side)

    near = [Group((near_sems.at[kind, 0], None)) for kind in (0, 1)]
    ring = [Group((ring_send.at[0, kind], rest_recv.at[kind])) for kind in (0, 1)]

    def forward(index):
        start, size = pieces[index]
        for kind in (0, 1):
            part = refs[kind].at[where[kind], pl.ds(start, size)]
            if start:
                settle(near_sems.at[kind, index], part)
            for way in (0, 1):
                ring[kind].start(
                    part, part, to_ring(kind, 2 - 4 * way), ring_recv.at[0, kind, way, index]
                )

    def onward(index):
        start, size = pieces[index]
        for kind in (0, 1):
            for way in (0, 1):
                sign = 1 - 2 * way
                part = refs[kind].at[block_at(kind, -2 * sign), pl.ds(start, size)]
                settle(ring_recv.at[0, kind, way, index], part)
                if (start < half) == (way == 0):
                    ring[kind].start(part, part, to_ring(kind, 2 * sign))
                ring[kind].start(part, part, to_ring(kind, sign))

    for offset in far_first(side):
        for kind in (0, 1):
            slot = slot_of(side - offset, side)
            near[kind].start(
                refs[kind].at[where[kind], 0],
                refs[kind].at[where[kind], slot],
                near_peer[kind](y, z, side, offset),
                near_sems.at[kind, 1 if slot < half else 2],
            )
    forward(0)
    across = Group((pair_sems.at[0, 0], pair_sems.at[0, 1]))
    for o in range(1, n_rcv):
        across.start(sgeo_ref.at[rcv], sgeo_ref.at[rcv], peer_r(rcv, n_rcv, o))

    settle(load_sem.at[1], act_ref)
    settle(load_sem.at[2], ids)
    ageo_ref[...] = turned(geometric(act_ref[0], act_ref[1]))

    send_row = jnp.sum(turned(jnp.exp(own_ref[2] - own_ref[3])), axis=0, keepdims=True)
    recv_row = jnp.sum(turned(jnp.exp(own_ref[0] - own_ref[1])), axis=0, keepdims=True)
    tot_src[0, 0:1] = send_row
    tot_src[0, 1:2] = recv_row

    def totals_in(level):
        settle(tot_sems.at[level, 1], tot_dst.at[level, pl.ds(0, (n_rcv, side, side)[level] - 1)])
        value = tot_dst[level, 0]
        for index in range(1, (n_rcv, side, side)[level]):
            value = value + tot_dst[level, index]
        return value

    def exchange_totals(level):
        if level:
            tot_src[level] = totals_in(level - 1)
        me = (rcv, y, z)[level]
        tot_dst[level, me] = tot_src[level]
        group = Group((tot_sems.at[level, 0], tot_sems.at[level, 1]))
        for o in range(1, (n_rcv, side, side)[level]):
            device = peer_r(rcv, n_rcv, o) if level == 0 else to_ring(level - 1, o)
            group.start(tot_src.at[level], tot_dst.at[level, me], device)

    def link(slot, carry):
        b, c = ids[0, 0, slot], ids[1, 0, slot]
        before_b, before_c = jnp.int32(slots), jnp.int32(slots)
        for other in range(slots):
            earlier = other < slot
            before_b = jnp.where((ids[0, 0, other] == b) & earlier, other, before_b)
            before_c = jnp.where((ids[1, 0, other] == c) & earlier, other, before_c)
        prev[0, slot] = before_b
        prev[1, slot] = before_c
        return carry

    def final(row, table):
        def body(block, carry):
            found = jnp.int32(slots)
            for other in range(slots):
                found = jnp.where(ids[row, 0, other] == block, other, found)
            table[block] = found
            return carry

        return body

    exchange_totals(0)
    lax.fori_loop(0, slots, link, 0)
    for index in range(1, len(pieces)):
        forward(index)
    exchange_totals(1)
    for index in range(len(pieces)):
        onward(index)
    for kind in (0, 1):
        part = refs[kind].at[where[kind]]
        for sign in (1, -1):
            ring[kind].start(part, part, to_ring(kind, sign))

    exchange_totals(2)
    settle(pair_sems.at[0, 1], sgeo_ref.at[pl.ds(0, n_rcv - 1)])

    def scale(slot, carry):
        b, a = ids[0, 0, slot], ids[2, 0, slot]
        sender = sgeo_ref[pl.ds(b * span, span)].reshape(edge, lanes)
        scaled = (sender.astype(f32) * ageo_ref[pl.ds(a, 1), :]).astype(bf16)
        scaled_ref[slot] = scaled
        turned_ref[slot] = scaled.T[:rank]
        return carry

    lax.fori_loop(0, slots, scale, 0, unroll=4)
    lax.fori_loop(0, blocks, final(1, last_recv), 0)
    lax.fori_loop(0, send_blocks, final(0, last_send), 0)
    act_chunk = actions // n_rcv
    send_slots[slots] = jnp.zeros(send_slots.shape[1:], f32)
    recv_slots[slots] = jnp.zeros(recv_slots.shape[1:], f32)
    settle(load_sem.at[3], fill)
    settle(load_sem.at[4], aid_row)
    settle(load_sem.at[5], counts)
    for kind in (0, 1):
        settle(rest_recv.at[kind], refs[kind].at[pl.ds(0, 5)])

    live_count = fill[0, 0]

    def recv_block(slot):
        begin = ids[1, 0, slot] * span
        ty, tz = begin // side, lax.rem(begin, side)
        down = slot_at(ty - y, side)
        return jnp.concatenate(
            [
                jnp.concatenate(
                    [top_ref[ty, slot_at(tz + e - z, side)] for e in range(span)], axis=1
                ),
                jnp.concatenate([low_ref[tz + e, down] for e in range(span)], axis=1),
            ],
            axis=0,
        )

    def padded(recv):
        return jnp.concatenate([recv, jnp.zeros((lanes - rank, edge), bf16)], axis=0)

    def ratio_tile(slot):
        live = jnp.where(slot < live_count, 1.0, 0.0).astype(f32)
        expected = jnp.dot(
            scaled_ref[slot], padded(recv_block(slot)), preferred_element_type=f32
        )
        return (counts[slot].astype(f32) * live / expected).astype(bf16)

    def ratio_group(group, carry):
        done = [ratio_tile(group * unroll + u) for u in range(unroll)]
        for u, ratios in enumerate(done):
            counts[group * unroll + u] = ratios
        return carry

    lax.fori_loop(0, slots // unroll, ratio_group, 0)

    def stat_tile(slot):
        recv, scaled, ratios = recv_block(slot), scaled_ref[slot], counts[slot]
        toward_send = lax.dot_general(
            ratios, padded(recv), (((1,), (1,)), ((), ())), preferred_element_type=f32
        )
        toward_recv = jnp.dot(turned_ref[slot], ratios, preferred_element_type=f32)
        send_term = scaled.astype(f32) * toward_send
        recv_term = recv.astype(f32) * toward_recv
        return send_term, recv_term, jnp.sum(send_term, axis=0, keepdims=True)

    def stat_group(group, carry):
        done = [stat_tile(group * unroll + u) for u in range(unroll)]
        for u, (send_term, recv_term, act_term) in enumerate(done):
            slot = group * unroll + u
            send_slots[slot] = send_term + send_slots[prev[0, slot]]
            recv_slots[slot] = recv_term + recv_slots[prev[1, slot]]
            act_rows[pl.ds(slot, 1), :] = act_term
        return carry

    lax.fori_loop(0, slots // unroll, stat_group, 0)

    action_id = lax.broadcasted_iota(jnp.int32, (actions, slots), 0)
    onehot = jnp.where(action_id == aid_row[...], 1.0, 0.0).astype(f32)
    act_sum = jnp.dot(
        onehot, act_rows[...], preferred_element_type=f32, precision=lax.Precision.HIGHEST
    )
    for chunk in range(n_rcv):
        act_own[chunk] = act_sum[chunk * act_chunk : (chunk + 1) * act_chunk].astype(bf16)
    acts = Group((pair_sems.at[1, 0], pair_sems.at[1, 1]))
    for o in range(1, n_rcv):
        other = lax.rem(rcv + o, n_rcv)
        acts.start(act_own.at[other], act_dst.at[rcv], {"rcv": other})
    act_dst[rcv] = act_own[rcv]

    def hand_over(kind, distance):
        line = block_at(kind, distance)
        if kind == 0:
            for block in range(side // span):
                table = last_recv[line * (side // span) + block]
                value = recv_slots[table, pl.ds(0, rows), :].astype(bf16)
                for e in range(span):
                    slot = slot_at(block * span + e - z, side)
                    parts[0, line, slot] = value[:, e * lanes : (e + 1) * lanes]
        else:
            block = line // span
            column = pl.multiple_of(lax.rem(line, span) * lanes, lanes)
            for ty in range(side):
                table = last_recv[ty * (side // span) + block]
                value = recv_slots[table, pl.ds(rows, rows), pl.ds(column, lanes)]
                parts[1, line, slot_at(ty - y, side)] = value.astype(bf16)

    def piece_of(kind, distance, start, size):
        return parts.at[kind, block_at(kind, distance), pl.ds(start, size)]

    out_ring = [Group((ring_send.at[1, kind], None)) for kind in (0, 1)]
    backwards = tuple(reversed(range(len(pieces))))

    def far_parts(index):
        start, size = pieces[index]
        for kind in (0, 1):
            for way in (0, 1):
                sign = 1 - 2 * way
                at = (kind, way, pl.ds(start, size))
                arrive = ring_recv.at[1, kind, way, index]
                if (start < half) == (way == 0):
                    out_ring[kind].start(
                        piece_of(kind, 4 * sign, start, size),
                        from4.at[at],
                        to_ring(kind, 2 * sign),
                        arrive,
                    )
                out_ring[kind].start(
                    piece_of(kind, 3 * sign, start, size), from3.at[at], to_ring(kind, sign), arrive
                )

    def join(index):
        start, size = pieces[index]
        for kind in (0, 1):
            for way in (0, 1):
                sign = 1 - 2 * way
                at = (kind, way, pl.ds(start, size))
                both = (start < half) == (way == 0)
                settle(
                    ring_recv.at[1, kind, way, index],
                    parts.at[0, 0, pl.ds(0, size * (2 if both else 1))],
                )
                total = parts[kind, block_at(kind, 2 * sign), pl.ds(start, size)].astype(f32)
                total = total + from3[at].astype(f32)
                if both:
                    total = total + from4[at].astype(f32)
                joined[at] = total.astype(bf16)
                out_ring[kind].start(
                    joined.at[at], from2.at[at], to_ring(kind, 2 * sign), done_recv.at[kind, index]
                )
        for kind in (0, 1):
            for way in (0, 1):
                sign = 1 - 2 * way
                out_ring[kind].start(
                    piece_of(kind, sign, start, size),
                    from1.at[kind, way, pl.ds(start, size)],
                    to_ring(kind, sign),
                    done_recv.at[kind, index],
                )

    def total_of(ref, count):
        value = ref[0].astype(f32)
        for index in range(1, count):
            value = value + ref[index].astype(f32)
        return value

    def spread(level, value):
        me = where[level]
        sum_src[level] = value.astype(bf16)
        sum_dst[level, me] = value.astype(bf16)
        group = Group((pair_sems.at[2 + level, 0], pair_sems.at[2 + level, 1]))
        for o in far_first(side):
            group.start(sum_src.at[level], sum_dst.at[level, me], to_ring(level, o))

    last = [Group((last_sems.at[kind, 0], last_sems.at[kind, 1])) for kind in (0, 1)]

    def finish(index):
        start, size = pieces[index]
        for kind in (0, 1):
            settle(done_recv.at[kind, index], parts.at[0, pl.ds(0, size), pl.ds(0, 4)])
            total = parts[kind, where[kind], pl.ds(start, size)].astype(f32)
            for way in (0, 1):
                at = (kind, way, pl.ds(start, size))
                total = total + from1[at].astype(f32) + from2[at].astype(f32)
            near_src[kind, pl.ds(start, size)] = total.astype(bf16)
            for offset in far_first(side):
                slot = slot_of(offset, side)
                if start <= slot < start + size:
                    last[kind].start(
                        near_src.at[kind, slot],
                        near_dst.at[kind, slot_of(side - offset, side)],
                        near_peer[kind](y, z, side, offset),
                    )

    for distance in (half, half - 1, 1 - half):
        for kind in (0, 1):
            hand_over(kind, distance)
    for index in backwards:
        far_parts(index)
    for distance in (2, -2):
        for kind in (0, 1):
            hand_over(kind, distance)
    settle(pair_sems.at[1, 1], act_dst.at[pl.ds(0, n_rcv - 1)])
    spread(0, total_of(act_dst, n_rcv))
    for distance in (1, -1):
        for kind in (0, 1):
            hand_over(kind, distance)
    join(backwards[0])
    join(backwards[1])
    settle(pair_sems.at[2, 1], sum_dst.at[0, pl.ds(0, side - 1)])
    spread(1, total_of(sum_dst.at[0], side))
    join(backwards[2])
    for kind in (0, 1):
        hand_over(kind, 0)

    def give(block, carry):
        value = send_slots[last_send[block]].astype(bf16)
        for e in range(span):
            send_part[block * span + e] = value[e * lanes : (e + 1) * lanes]
        return carry

    lax.fori_loop(0, send_blocks, give, 0)
    sends = Group((pair_sems.at[4, 0], pair_sems.at[4, 1]))
    for o in range(1, n_rcv):
        other = lax.rem(rcv + o, n_rcv)
        sends.start(send_part.at[other], send_dst.at[rcv], {"rcv": other})
    send_dst[rcv] = send_part[rcv]

    finish(backwards[0])
    finish(backwards[1])
    settle(pair_sems.at[3, 1], sum_dst.at[1, pl.ds(0, side - 1)])
    act_out[pl.ds(rcv * act_chunk, act_chunk), :] = total_of(sum_dst.at[1], side)
    own = act_out.at[pl.ds(rcv * act_chunk, act_chunk), :]
    back = Group((pair_sems.at[5, 0], pair_sems.at[5, 1]))
    for o in range(1, n_rcv):
        back.start(own, own, peer_r(rcv, n_rcv, o))
    finish(backwards[2])
    for kind in (0, 1):
        near_dst[kind, 0] = near_src[kind, 0]
    tot_out[...] = totals_in(2)
    settle(pair_sems.at[4, 1], send_dst.at[pl.ds(0, n_rcv - 1)])
    send_out[...] = total_of(send_dst, n_rcv)

    for kind in (0, 1):
        settle(near_sems.at[kind, 0], refs[kind].at[0, pl.ds(0, side - 1)])
        settle(ring_send.at[0, kind], refs[kind].at[pl.ds(0, side - 1)])
        settle(ring_send.at[1, kind], refs[kind].at[pl.ds(0, side - 1)])
    for level in range(3):
        like = tot_dst.at[level, pl.ds(0, (n_rcv, side, side)[level] - 1)]
        settle(tot_sems.at[level, 0], like)
    settle(pair_sems.at[0, 0], sgeo_ref.at[pl.ds(0, n_rcv - 1)])
    settle(pair_sems.at[1, 0], act_dst.at[pl.ds(0, n_rcv - 1)])
    settle(pair_sems.at[2, 0], sum_dst.at[0, pl.ds(0, side - 1)])
    settle(pair_sems.at[3, 0], sum_dst.at[1, pl.ds(0, side - 1)])
    settle(pair_sems.at[4, 0], send_dst.at[pl.ds(0, n_rcv - 1)])
    for kind in (0, 1):
        settle(last_sems.at[kind, 1], near_dst.at[kind, pl.ds(0, side - 1)])
        recv_out[kind * rows : (kind + 1) * rows] = total_of(near_dst.at[kind], side)
    for kind in (0, 1):
        settle(last_sems.at[kind, 0], near_dst.at[kind, pl.ds(0, side - 1)])
    for end in (1, 0):
        settle(pair_sems.at[5, end], act_out.at[pl.ds(0, (n_rcv - 1) * act_chunk), :])


def refresh_kernel(*refs):
    sources, outs, refs = refs[:10], refs[10:16], refs[16:]
    held, load_sem = refs[:10], refs[10]
    for index in range(10):
        pltpu.make_async_copy(sources[index], held[index], load_sem.at[index]).start()
    for index in range(10):
        pltpu.make_async_copy(sources[index], held[index], load_sem.at[index]).wait()
    ss_ref, sr_ref, rs_ref, rr_ref, as_ref, ar_ref, send_ref, recv_ref, act_ref, tot_ref = held
    ss_out, sr_out, rs_out, rr_out, as_out, ar_out = outs
    rank = as_ref.shape[0]
    row = lax.broadcasted_iota(jnp.int32, (rank, lanes), 0)
    col = lax.broadcasted_iota(jnp.int32, (rank, lanes), 1)

    def column(index):
        wide = jnp.broadcast_to(tot_ref[pl.ds(index, 1), :], (rank, lanes))
        return jnp.sum(jnp.where(row == col, wide, 0.0), axis=1, keepdims=True)

    send_total, recv_total = column(0), column(1)
    act_total = jnp.sum(jnp.exp(as_ref[...] - ar_ref[...]), axis=1, keepdims=True)
    ss_out[0] = refresh(ss_ref[0], prior_shape + send_ref[...].T[:rank])
    sr_out[0] = refresh(sr_ref[0], prior_rate + recv_total * act_total)
    rs_out[0] = refresh(rs_ref[0], prior_shape + recv_ref[...])
    rr_out[0] = refresh(rr_ref[0], prior_rate + send_total * act_total)
    as_out[...] = refresh(as_ref[...], prior_shape + act_ref[...].T[:rank])
    ar_out[...] = refresh(ar_ref[...], prior_rate + send_total * recv_total)


def per_device(
    side,
    n_rcv,
    tile_counts,
    tile_sender,
    tile_receiver,
    tile_action,
    tile_fill,
    ss,
    sr,
    rs,
    rr,
    ash,
    art,
):
    rank, actions = ash.shape
    slots, edge = tile_counts.shape[2], tile_counts.shape[3]
    rows, span = rank // 2, edge // lanes
    blocks, send_blocks = side * side // span, n_rcv // span
    vmem = pl.BlockSpec(memory_space=pltpu.VMEM)
    hbm = pl.BlockSpec(memory_space=pltpu.HBM)
    shape = jax.ShapeDtypeStruct
    dma = pltpu.SemaphoreType.DMA
    geo = pltpu.VMEM((side, side, rows, lanes), bf16)
    landing = pltpu.VMEM((2, 2, side, rows, lanes), bf16)
    near = pltpu.VMEM((2, side, rows, lanes), bf16)
    sender = pltpu.VMEM((n_rcv, lanes, lanes), bf16)
    chunk = actions // n_rcv

    recv_stat, send_stat, act_stat, totals = pl.pallas_call(
        functools.partial(fused_kernel, side, n_rcv),
        out_shape=(
            shape((rank, lanes), f32),
            shape((lanes, lanes), f32),
            shape((actions, lanes), f32),
            shape((2, lanes), f32),
        ),
        in_specs=[hbm] * 11,
        out_specs=(vmem,) * 4,
        scratch_shapes=[
            pltpu.VMEM((4, rank, lanes), f32),
            pltpu.VMEM((2, rank, actions), f32),
            pltpu.SMEM((3, 1, slots), jnp.int32),
            pltpu.SMEM(tile_fill.shape, jnp.int32),
            pltpu.VMEM((1, slots), jnp.int32),
            pltpu.SMEM((2, slots), jnp.int32),
            pltpu.SMEM((blocks,), jnp.int32),
            pltpu.SMEM((send_blocks,), jnp.int32),
            pltpu.VMEM((slots, edge, edge), bf16),
            geo,
            geo,
            sender,
            pltpu.VMEM((actions, lanes), f32),
            pltpu.VMEM((slots, edge, lanes), bf16),
            pltpu.VMEM((slots, rank, edge), bf16),
            pltpu.VMEM((slots + 1, edge, lanes), f32),
            pltpu.VMEM((slots + 1, rank, edge), f32),
            pltpu.VMEM((slots, lanes), f32),
            pltpu.VMEM((2, side, side, rows, lanes), bf16),
            landing,
            landing,
            landing,
            landing,
            landing,
            near,
            near,
            sender,
            sender,
            pltpu.VMEM((n_rcv, chunk, lanes), bf16),
            pltpu.VMEM((n_rcv, chunk, lanes), bf16),
            pltpu.VMEM((2, chunk, lanes), bf16),
            pltpu.VMEM((2, side, chunk, lanes), bf16),
            pltpu.VMEM((3, 2, lanes), f32),
            pltpu.VMEM((3, max(side, n_rcv), 2, lanes), f32),
            dma((6,)),
            dma((2, 3)),
            dma((2, 2)),
            dma((2, 2, 2, 3)),
            dma((2,)),
            dma((2, 3)),
            dma((2, 2)),
            dma((6, 2)),
            dma((3, 2)),
        ],
        compiler_params=pltpu.CompilerParams(
            collective_id=0, has_side_effects=True, vmem_limit_bytes=whole_vmem
        ),
    )(
        tile_counts,
        tile_sender,
        tile_receiver,
        tile_action,
        tile_fill,
        ss,
        sr,
        rs,
        rr,
        ash,
        art,
    )

    sources = (ss, sr, rs, rr, ash, art, send_stat, recv_stat, act_stat, totals)
    return pl.pallas_call(
        refresh_kernel,
        out_shape=tuple(shape(x.shape, f32) for x in (ss, sr, rs, rr, ash, art)),
        in_specs=[hbm] * len(sources),
        out_specs=(vmem,) * 6,
        scratch_shapes=[pltpu.VMEM(x.shape, f32) for x in sources] + [dma((len(sources),))],
        compiler_params=pltpu.CompilerParams(vmem_limit_bytes=whole_vmem),
    )(*sources)


def solution(mesh):
    n_snd, n_rcv = mesh.shape["snd"], mesh.shape["rcv"]
    side = round(n_snd**0.5)
    return jax.shard_map(
        functools.partial(per_device, side, n_rcv),
        mesh=mesh,
        in_specs=(
            P("snd", "rcv", None, None, None),
            P("snd", "rcv", None),
            P("snd", "rcv", None),
            P("snd", "rcv", None),
            P("snd", "rcv"),
            P("snd", None, "rcv"),
            P("snd", None, "rcv"),
            P("rcv", None, "snd"),
            P("rcv", None, "snd"),
            P(),
            P(),
        ),
        out_specs=(
            P("snd", None, "rcv"),
            P("snd", None, "rcv"),
            P("rcv", None, "snd"),
            P("rcv", None, "snd"),
            P(),
            P(),
        ),
        check_vma=False,
    )
```
